32 devices in a mesh: band: 16 (over z, y, core), fft: 2 (over x).
Axes of the slice: x: 2, y: 2, z: 4, core: 2. Of those that a mesh axis runs over, the one named last changes fastest.
Arguments:
- orbitals: float32 [32, 128, 128, 128], P('band', 'fft'), may hold values from -6 to 6
- owners: int32 [1], replicated, may hold values from 0 to 15
- local_pick: int32 [16, 1], P('band'), may hold values from 0 to 1
Outputs:
- exchange_term: float32 [16, 128, 128, 128], P('band', 'fft')
The draws below stay inside these ranges and needn't reach their ends.
All inputs are finite; a program needn't handle non-finite values.
Results may differ from the reference program's by a relative error of at most 0.0003.
Values sent between devices are 32-bit elements; how exact they have to be, the bound alone decides.
No kernel may reach another device: no remote copies, remote signals or barrier semaphores. Data moves between devices by JAX's collectives and lax.ppermute only.
A program may use at most 128 MiB of HBM per device.

```python
import math
import jax
import jax.numpy as jnp
from jax import lax

NG = 128
ORB_DEV = 2
LOC = 1
ROUNDS = 1
BANDS = 32
N_BAND = 16


def plant(values, key, smallest, top_value):
    index_at = [jax.random.randint(jax.random.fold_in(key, axis), (), 0, length) for axis, length in enumerate(values.shape)]
    main_axis = values.shape.index(max(values.shape))
    neighbour = index_at[:main_axis] + [(index_at[main_axis] + 1) % values.shape[main_axis]] + index_at[main_axis + 1:]
    return values.at[tuple(index_at)].set(smallest).at[tuple(neighbour)].set(top_value)


def level_of(own_key, dims, split, low, high):
    def one(dim, shards_of):
        heights = jax.random.uniform(jax.random.fold_in(jax.random.fold_in(own_key, 6), dim), (shards_of,), jnp.float32, low / len(split), high / len(split))
        return jnp.repeat(jnp.exp(heights), dims[dim] // shards_of).reshape((-1,) + (1,) * (len(dims) - dim - 1))

    factor_of = one(*split[0])
    for cut in split[1:]:
        factor_of = factor_of * one(*cut)
    return factor_of


def centred(stream_key, extent, deviation, bound, shards=(), kind=jnp.bfloat16):
    values = deviation * jax.random.normal(stream_key, extent, jnp.float32)
    if shards:
        values = values * level_of(stream_key, extent, shards, -0.22, 0.18)
    return jnp.clip(values, -bound, bound).astype(kind)


def setup_inputs(seed: int = 0) -> dict:
    key_list = jax.random.split(jax.random.key(seed), 4)
    orbitals = centred(key_list[0], (BANDS, NG, NG, NG), 1.0, 6.0, ((0, 16), (1, 2)), jnp.float32)
    owners = jax.random.randint(key_list[1], (ROUNDS,), 0, N_BAND).astype(jnp.int32)
    local_pick = plant(jax.random.randint(key_list[2], (N_BAND, LOC), 0, ORB_DEV), jax.random.fold_in(key_list[2], 1), 0, ORB_DEV - 1).astype(jnp.int32)
    return dict(orbitals=orbitals, owners=owners, local_pick=local_pick)


def signed_freq(size):
    index = jnp.arange(size)
    return jnp.where(index < size // 2, index, index - size).astype(jnp.float32)

def coulomb_table():
    freq = signed_freq(NG)
    square = freq[:, None, None] ** 2 + freq[None, :, None] ** 2 + freq[None, None, :] ** 2
    scale = 0.25 * NG * math.sqrt(NG)
    return jnp.where(square > 0, scale / jnp.maximum(square, 1.0), 0.0)

def reference(orbitals, owners, local_pick):
    coulomb = coulomb_table()
    groups = jnp.arange(N_BAND, dtype=jnp.int32)[:, None]
    picked = (groups * ORB_DEV + local_pick).reshape(-1).astype(jnp.int32)
    sent_all = []
    for step in range(ROUNDS):
        start = (owners[step] * ORB_DEV).astype(jnp.int32)
        sent_all.append(lax.dynamic_slice_in_dim(orbitals, start, ORB_DEV, 0))

    def one_band(index):
        selected = lax.dynamic_index_in_dim(orbitals, index, 0, keepdims=False)
        total = jnp.zeros(selected.shape, jnp.float32)
        for sent in sent_all:
            for orbit in range(ORB_DEV):
                partner = sent[orbit]
                density = partner * selected
                potential = jnp.real(jnp.fft.ifftn(jnp.fft.fftn(density) * coulomb))
                total = total + potential * partner
        return total
    return lax.map(one_band, picked)
```

```python
import functools
import math

import jax
import jax.numpy as jnp
import ml_dtypes
import numpy as np
from jax import lax
from jax.experimental import pallas as pl
from jax.experimental.pallas import tpu as pltpu
from jax.sharding import PartitionSpec as P

F32 = jnp.float32
BF16 = jnp.bfloat16
ROWS = 8
CHUNKS = 8
GROUPS = ((0, 4), (4, 6), (6, 8))


def spread(shard, axis, root):
    mine = lax.axis_index(axis) == root
    return lax.psum(jnp.where(mine, shard, jnp.zeros_like(shard)), axis)


def dft_tables(size):
    index = jnp.arange(size, dtype=jnp.int32)
    product = index[:, None] * index[None, :] % size
    angle = product.astype(jnp.float32) * (2.0 * math.pi / size)
    return (jnp.cos(angle), jnp.sin(angle))


def signed_freq(index, size):
    return jnp.where(index < size // 2, index, index - size).astype(jnp.float32)


def along(form, data, table):
    return jnp.einsum(form, data, table, precision=lax.Precision.HIGHEST)


def transform(density, cosine, sine, kernel):
    last_form = "pzxy,yk->pzxk"
    middle_form = "pzxy,xk->pzky"
    first_form = "pzab,zk->pkab"
    evens = density[0::2]
    odds = density[1::2]
    real_part = along(last_form, evens, cosine) + along(last_form, odds, sine)
    imag_part = along(last_form, odds, cosine) - along(last_form, evens, sine)
    mixed_real = along(middle_form, real_part, cosine) + along(middle_form, imag_part, sine)
    mixed_imag = along(middle_form, imag_part, cosine) - along(middle_form, real_part, sine)
    line_real = lax.all_to_all(mixed_real, "fft", split_axis=2, concat_axis=1, tiled=True)
    line_imag = lax.all_to_all(mixed_imag, "fft", split_axis=2, concat_axis=1, tiled=True)
    spec_real = along(first_form, line_real, cosine) + along(first_form, line_imag, sine)
    spec_imag = along(first_form, line_imag, cosine) - along(first_form, line_real, sine)
    spec_real = spec_real * kernel
    spec_imag = spec_imag * kernel
    back_real = along(first_form, spec_real, cosine) - along(first_form, spec_imag, sine)
    back_imag = along(first_form, spec_imag, cosine) + along(first_form, spec_real, sine)
    slab_real = lax.all_to_all(back_real, "fft", split_axis=1, concat_axis=2, tiled=True)
    slab_imag = lax.all_to_all(back_imag, "fft", split_axis=1, concat_axis=2, tiled=True)
    inner_real = along(middle_form, slab_real, cosine) - along(middle_form, slab_imag, sine)
    inner_imag = along(middle_form, slab_imag, cosine) + along(middle_form, slab_real, sine)
    first_field = along(last_form, inner_real, cosine) - along(last_form, inner_imag, sine)
    second_field = along(last_form, inner_imag, cosine) + along(last_form, inner_real, sine)
    return jnp.stack([first_field, second_field], 1).reshape(density.shape)


def general(orbitals, owners, local_pick):
    grid = orbitals.shape[-1]
    cosine, sine = dft_tables(grid)
    groups = lax.axis_size("fft")
    width = grid // groups
    start = lax.axis_index("fft") * width
    freq_first = signed_freq(jnp.arange(grid, dtype=jnp.int32), grid)
    freq_second = signed_freq(start + jnp.arange(width, dtype=jnp.int32), grid)
    square = (
        freq_first[:, None, None] ** 2
        + freq_second[None, :, None] ** 2
        + freq_first[None, None, :] ** 2
    )
    scale = 0.25 * grid * math.sqrt(grid) / (grid * grid * grid)
    kernel = jnp.where(square > 0, scale / jnp.maximum(square, 1.0), 0.0)
    selected = jnp.take(orbitals, local_pick[0], axis=0)
    grid_shape = selected.shape[1:]
    total = jnp.zeros_like(selected)
    for step in range(owners.shape[0]):
        sent = spread(orbitals, "band", owners[step])
        density = (sent[:, None] * selected[None]).reshape((-1,) + grid_shape)
        potentials = transform(density, cosine, sine, kernel)
        shaped = potentials.reshape((sent.shape[0], selected.shape[0]) + grid_shape)
        total = total + jnp.sum(shaped * sent[:, None], axis=0)
    return total


def host_tables(grid):
    index = np.arange(grid)
    angle = 2.0 * np.pi * (np.outer(index, index) % grid) / grid
    return np.cos(angle), np.sin(angle)


def as_pair(table):
    high = table.astype(ml_dtypes.bfloat16)
    low = (table - high.astype(np.float64)).astype(ml_dtypes.bfloat16)
    return jnp.asarray(high), jnp.asarray(low)


def blocks(a, b, c, d):
    return np.block([[a, b], [c, d]])


def plane_order(core, half, part):
    base = np.arange(half).reshape(-1, 2, part)
    if core:
        base = base[:, ::-1]
    return core * half + base.reshape(-1)


def tables(grid, part):
    cos, sin = host_tables(grid)
    half = grid // 2
    columns = [np.arange(grid), np.concatenate([np.arange(half, grid), np.arange(half)])]
    slabs = [plane_order(core, half, part) for core in range(2)]
    depths = [np.concatenate([slabs[core], slabs[1 - core]]) for core in range(2)]

    def to_spectrum(order):
        c, s = cos[order], sin[order]
        return blocks(c, s, -s, c)

    def from_planes(order):
        c, s = cos[:, order], sin[:, order]
        return blocks(c, s, -s, c)

    def to_planes(order):
        c, s = cos[order], sin[order]
        return blocks(c, -s, s, c)

    def from_spectrum(order):
        c, s = cos[:, order], sin[:, order]
        return blocks(c, -s, s, c)

    both = dict(
        last_fwd=blocks(cos, -sin, sin, cos),
        last_inv=blocks(cos, sin, -sin, cos),
        mid_fwd=np.stack([to_spectrum(order) for order in columns]),
        mid_inv=np.stack([from_spectrum(order) for order in columns]),
        first_fwd=np.stack([from_planes(order) for order in depths]),
        first_inv=np.stack([to_planes(order) for order in depths]),
    )
    return {name: as_pair(value) for name, value in both.items()}


def split(value):
    high = value.astype(BF16)
    return high, (value - high.astype(F32)).astype(BF16)


def mm(a, b):
    return jnp.dot(a, b, preferred_element_type=F32)


def right(data, high, low):
    top, rest = split(data)
    return mm(top, high) + (mm(rest, high) + mm(top, low))


def left(high, low, data):
    top, rest = split(data)
    return mm(high, top) + (mm(high, rest) + mm(low, top))


def forward_body(info, phi, own0, own1, other0, other1, wyh, wyl, wxh, wxl, keep, send):
    grid = phi.shape[-1]
    half = grid // 2
    rows = phi.shape[0]
    part = rows // 2
    core = info[0]
    near = phi[pl.ds(core * part, part)]
    far = phi[pl.ds((1 - core) * part, part)]
    re = jnp.concatenate([near * own0[...], far * other0[...]], axis=0)
    im = jnp.concatenate([near * own1[...], far * other1[...]], axis=0)
    data = jnp.concatenate([re, im], axis=-1).reshape(rows * grid, 2 * grid)
    lines = right(data, wyh[...], wyl[...])
    for first in range(0, rows, 2):
        planes = []
        for z in (first, first + 1):
            plane = lines[z * grid : (z + 1) * grid]
            planes.append(jnp.concatenate([plane[:, :grid], plane[:, grid:]], axis=0))
        out = left(wxh[0], wxl[0], jnp.concatenate(planes, axis=1))
        for pos, z in enumerate((first, first + 1)):
            plane = out[:, pos * grid : (pos + 1) * grid]
            for comp in range(2):
                base = comp * grid
                keep[comp, :, z, :] = plane[base : base + half]
                send[comp, :, z, :] = plane[base + half : base + grid]


def middle_body(info, *refs):
    count = (len(refs) - 4) // 4
    keeps, recvs = refs[:count], refs[count : 2 * count]
    wfh, wfl, wih, wil = refs[2 * count : 2 * count + 4]
    keep_outs, send_outs = refs[2 * count + 4 : 3 * count + 4], refs[3 * count + 4 :]
    rows = keeps[0].shape[1]
    grid = keeps[0].shape[-1]
    half = grid // 2
    scale = 0.25 * grid * math.sqrt(grid) / (grid * grid * grid)
    kz = lax.broadcasted_iota(jnp.int32, (grid, grid), 0)
    ky = lax.broadcasted_iota(jnp.int32, (grid, grid), 1)
    fz = jnp.where(kz < grid // 2, kz, kz - grid)
    fy = jnp.where(ky < grid // 2, ky, ky - grid)
    plane_square = fz * fz + fy * fy
    start = info[0] * half + pl.program_id(0) * rows
    lane = lax.broadcasted_iota(jnp.int32, (1, grid), 1)
    for first in range(0, rows, 2):
        planes = []
        for k in (first, first + 1):
            for comp in range(2):
                pieces = [ref[comp, k] for ref in keeps + recvs]
                if k == 0:
                    drop = jnp.where((lane == 0) & (start == 0), pieces[0][0:1], 0.0)
                    pieces = [piece - drop for piece in pieces]
                planes.append(jnp.concatenate(pieces, axis=0))
        data = jnp.concatenate(
            [
                jnp.concatenate(planes[:2], axis=0),
                jnp.concatenate(planes[2:], axis=0),
            ],
            axis=1,
        )
        spec = left(wfh[0], wfl[0], data)
        factors = []
        for k in (first, first + 1):
            kx = start + k
            fx = jnp.where(kx < grid // 2, kx, kx - grid)
            square = (plane_square + fx * fx).astype(F32)
            factors.append(jnp.where(square > 0, scale / jnp.maximum(square, 1.0), 0.0))
        factor = jnp.concatenate(factors, axis=1)
        spec = spec * jnp.concatenate([factor, factor], axis=0)
        out = left(wih[0], wil[0], spec)
        for pos, k in enumerate((first, first + 1)):
            plane = out[:, pos * grid : (pos + 1) * grid]
            for comp in range(2):
                row = comp * grid
                for ref in keep_outs + send_outs:
                    size = ref.shape[2]
                    ref[comp, k] = plane[row : row + size]
                    row += size


def backward_body(info, keep, recv, own0, own1, other0, other1, wxh, wxl, wyh, wyl, out):
    grid = keep.shape[-1]
    rows = keep.shape[2]
    part = rows // 2
    core = info[0]
    lines = []
    for first in range(0, rows, 2):
        planes = []
        for z in (first, first + 1):
            planes.append(
                jnp.concatenate(
                    [keep[0, :, z, :], recv[0, :, z, :], keep[1, :, z, :], recv[1, :, z, :]],
                    axis=0,
                )
            )
        mixed = left(wxh[0], wxl[0], jnp.concatenate(planes, axis=1))
        for pos in range(2):
            plane = mixed[:, pos * grid : (pos + 1) * grid]
            lines.append(jnp.concatenate([plane[:grid], plane[grid:]], axis=1))
    fields = right(jnp.concatenate(lines, axis=0), wyh[...], wyl[...])
    re = fields[:, :grid].reshape(rows, grid, grid)
    im = fields[:, grid:].reshape(rows, grid, grid)
    out[pl.ds(core * part, part)] = re[:part] * own0[...] + im[:part] * own1[...]
    out[pl.ds((1 - core) * part, part)] = re[part:] * other0[...] + im[part:] * other1[...]


def call(body, grid_size, in_specs, out_specs, out_shape):
    return pl.pallas_call(
        body,
        grid_spec=pltpu.PrefetchScalarGridSpec(
            num_scalar_prefetch=1,
            grid=(grid_size,),
            in_specs=in_specs,
            out_specs=out_specs,
        ),
        out_shape=out_shape,
        compiler_params=pltpu.CompilerParams(vmem_limit_bytes=24 * 1024 * 1024),
    )


def paired(orbitals, owners, local_pick):
    n_orb, half, grid, _ = orbitals.shape
    bands = lax.axis_size("band")
    chips = bands // 2
    layers = chips // 2
    band = lax.axis_index("band")
    x = lax.axis_index("fft")
    core = band % 2
    chip = band // 2
    y = chip % 2
    home = core == x
    axes = ("band", "fft")

    def at(chip_, core_, x_):
        return (chip_ * 2 + core_) * 2 + x_

    def move(value, pairs):
        return lax.ppermute(value, axes, pairs)

    spots = [(t, c, p) for t in range(chips) for c in range(2) for p in range(2)]
    cross = [(at(t, c, p), at(t, p, c)) for t, c, p in spots if c != p]
    sibling = [(at(t, c, p), at(t, 1 - c, p)) for t, c, p in spots]
    over_x = [(at(t, c, p), at(t, c, 1 - p)) for t, c, p in spots]
    over_y = [(at(t, c, p), at(t ^ 1, c, p)) for t, c, p in spots]
    cycle = [2 * z for z in range(layers)] + [2 * z + 1 for z in reversed(range(layers))]
    length = len(cycle)
    after = {cycle[i]: cycle[(i + 1) % length] for i in range(length)}
    before = {chip_: source for source, chip_ in after.items()}
    around = [
        [(at(t, c, p), at(follow[t], c, p)) for t, c, p in spots] for follow in (after, before)
    ]
    place = jnp.asarray(np.argsort(np.array(cycle)).astype(np.int32))

    pick = local_pick[0, 0]
    owner = owners[0]
    own_chip = owner // 2
    own_here = chip == own_chip
    direct = (owner % 2) == core
    ahead = jnp.mod(place[chip] - place[own_chip], length)
    behind = jnp.mod(place[own_chip] - place[chip], length)
    distance = (ahead, behind)

    planes = half // CHUNKS
    part = planes // 2
    near = [move(orbitals[:, :planes], sibling), move(orbitals, sibling)]
    chosen_orbital = lax.dynamic_index_in_dim(orbitals, pick, 0, keepdims=False)
    phi = jnp.where(home, chosen_orbital, move(chosen_orbital, cross))

    def injected(s, k):
        start = k * planes + core * part
        own = lax.dynamic_slice_in_dim(orbitals[s], start, part, 0)
        other = lax.dynamic_slice_in_dim(near[min(k, 1)][s], start, part, 0)
        return jnp.where(direct, own, other)

    steps = CHUNKS + length - 2
    ring = [jnp.zeros(((CHUNKS + 1) * part, grid, grid), F32) for _ in range(2)]
    carried = [None, None]
    pieces = []
    for t in range(steps + 1):
        for s in range(2):
            held = carried[s]
            if t < CHUNKS:
                fresh = injected(s, t)
                held = fresh if held is None else jnp.where(own_here, fresh, held)
            k = t - distance[s]
            slot = jnp.where((k >= 0) & (k < CHUNKS), k, CHUNKS)
            ring[s] = lax.dynamic_update_slice(ring[s], held, (slot * part, 0, 0))
            if t < steps:
                carried[s] = move(held, around[s])
        for lo, hi in GROUPS:
            if hi - 1 + length - 1 == t:
                local = [ring[s][lo * part : hi * part] for s in range(2)]
                got = move(jnp.where(y == 0, local[0], local[1]), over_x)
                also = move(got, over_y)
                hop = [jnp.where(y == s, got, also) for s in range(2)]
                own = [jnp.where(home, local[s], hop[s]) for s in range(2)]
                other = [move(jnp.where(home, hop[s], local[s]), sibling) for s in range(2)]
                pieces.append(own + other)

    info = core.astype(jnp.int32)[None]
    table = tables(grid, part)

    def whole(shape):
        return pl.BlockSpec(shape, lambda i, info: (0,) * len(shape))

    def chosen(shape):
        return pl.BlockSpec((1,) + shape, lambda i, info: (info[0],) + (0,) * len(shape))

    square = (2 * grid, 2 * grid)
    quarter = pl.BlockSpec((part, grid, grid), lambda i, info: (i, 0, 0))
    lines = pl.BlockSpec((2, half, planes, grid), lambda i, info: (0, 0, i, 0))
    keeps, sends = [], []
    for (lo, hi), piece in zip(GROUPS, pieces):
        spectrum = jax.ShapeDtypeStruct((2, half, (hi - lo) * planes, grid), F32)
        keep, send = call(
            forward_body,
            hi - lo,
            [pl.BlockSpec((planes, grid, grid), lambda i, info, lo=lo: (lo + i, 0, 0))]
            + [quarter] * 4
            + [whole(square)] * 2
            + [chosen(square)] * 2,
            [lines, lines],
            [spectrum, spectrum],
        )(info, phi, *piece, *table["last_fwd"], *table["mid_fwd"])
        keeps.append(keep)
        sends.append(send)
    recvs = [move(send, sibling) for send in sends]
    cols = [
        pl.BlockSpec((2, ROWS, (hi - lo) * planes, grid), lambda i, info: (0, i, 0, 0))
        for lo, hi in GROUPS
    ]
    shapes = [jax.ShapeDtypeStruct(keep.shape, F32) for keep in keeps]
    results = call(
        middle_body,
        half // ROWS,
        cols * 2 + [chosen(square)] * 4,
        cols * 2,
        shapes * 2,
    )(info, *keeps, *recvs, *table["first_fwd"], *table["first_inv"])
    keeps, sends = results[: len(GROUPS)], results[len(GROUPS) :]
    recvs = [move(send, sibling) for send in sends]
    terms = []
    for (lo, hi), piece, keep, recv in zip(GROUPS, pieces, keeps, recvs):
        term = call(
            backward_body,
            hi - lo,
            [lines, lines]
            + [quarter] * 4
            + [chosen(square)] * 2
            + [whole(square)] * 2,
            pl.BlockSpec((planes, grid, grid), lambda i, info: (i, 0, 0)),
            jax.ShapeDtypeStruct(((hi - lo) * planes, grid, grid), F32),
        )(info, keep, recv, *piece, *table["mid_inv"], *table["last_inv"])
        terms.append(jnp.where(home, term, move(term, cross)))
    return jnp.concatenate(terms, axis=0)[None]


def solution(mesh):
    in_specs = (P("band", "fft", None, None), P(), P("band", None))
    out_specs = P("band", "fft", None, None)
    two_slabs = mesh.shape["fft"] == 2 and mesh.shape["band"] % 4 == 0

    def on_device(orbitals, owners, local_pick):
        fits = (
            orbitals.shape[0] == 2
            and orbitals.shape[1] == CHUNKS * ROWS
            and orbitals.shape[-1] % 128 == 0
            and owners.shape[0] == 1
            and local_pick.shape == (1, 1)
        )
        if two_slabs and fits:
            return paired(orbitals, owners, local_pick)
        return general(orbitals, owners, local_pick)

    return jax.shard_map(
        on_device, mesh=mesh, in_specs=in_specs, out_specs=out_specs, check_vma=False
    )
```

```python
import functools
import math

import jax
import jax.numpy as jnp
import ml_dtypes
import numpy as np
from jax import lax
from jax.experimental import pallas as pl
from jax.experimental.pallas import tpu as pltpu
from jax.sharding import PartitionSpec as P

F32 = jnp.float32
BF16 = jnp.bfloat16
ROWS = 8
CHUNKS = 8
GROUPS = ((0, 4), (4, 6), (6, 8))
TERM_GROUPS = ((0, 2), (2, 4), (4, 6), (6, 8))
HOP_STEPS = 2
PHI_STEP = 6


def spread(shard, axis, root):
    mine = lax.axis_index(axis) == root
    return lax.psum(jnp.where(mine, shard, jnp.zeros_like(shard)), axis)


def dft_tables(size):
    index = jnp.arange(size, dtype=jnp.int32)
    product = index[:, None] * index[None, :] % size
    angle = product.astype(jnp.float32) * (2.0 * math.pi / size)
    return (jnp.cos(angle), jnp.sin(angle))


def signed_freq(index, size):
    return jnp.where(index < size // 2, index, index - size).astype(jnp.float32)


def along(form, data, table):
    return jnp.einsum(form, data, table, precision=lax.Precision.HIGHEST)


def transform(density, cosine, sine, kernel):
    last_form = "pzxy,yk->pzxk"
    middle_form = "pzxy,xk->pzky"
    first_form = "pzab,zk->pkab"
    evens = density[0::2]
    odds = density[1::2]
    real_part = along(last_form, evens, cosine) + along(last_form, odds, sine)
    imag_part = along(last_form, odds, cosine) - along(last_form, evens, sine)
    mixed_real = along(middle_form, real_part, cosine) + along(middle_form, imag_part, sine)
    mixed_imag = along(middle_form, imag_part, cosine) - along(middle_form, real_part, sine)
    line_real = lax.all_to_all(mixed_real, "fft", split_axis=2, concat_axis=1, tiled=True)
    line_imag = lax.all_to_all(mixed_imag, "fft", split_axis=2, concat_axis=1, tiled=True)
    spec_real = along(first_form, line_real, cosine) + along(first_form, line_imag, sine)
    spec_imag = along(first_form, line_imag, cosine) - along(first_form, line_real, sine)
    spec_real = spec_real * kernel
    spec_imag = spec_imag * kernel
    back_real = along(first_form, spec_real, cosine) - along(first_form, spec_imag, sine)
    back_imag = along(first_form, spec_imag, cosine) + along(first_form, spec_real, sine)
    slab_real = lax.all_to_all(back_real, "fft", split_axis=1, concat_axis=2, tiled=True)
    slab_imag = lax.all_to_all(back_imag, "fft", split_axis=1, concat_axis=2, tiled=True)
    inner_real = along(middle_form, slab_real, cosine) - along(middle_form, slab_imag, sine)
    inner_imag = along(middle_form, slab_imag, cosine) + along(middle_form, slab_real, sine)
    first_field = along(last_form, inner_real, cosine) - along(last_form, inner_imag, sine)
    second_field = along(last_form, inner_imag, cosine) + along(last_form, inner_real, sine)
    return jnp.stack([first_field, second_field], 1).reshape(density.shape)


def general(orbitals, owners, local_pick):
    grid = orbitals.shape[-1]
    cosine, sine = dft_tables(grid)
    groups = lax.axis_size("fft")
    width = grid // groups
    start = lax.axis_index("fft") * width
    freq_first = signed_freq(jnp.arange(grid, dtype=jnp.int32), grid)
    freq_second = signed_freq(start + jnp.arange(width, dtype=jnp.int32), grid)
    square = (
        freq_first[:, None, None] ** 2
        + freq_second[None, :, None] ** 2
        + freq_first[None, None, :] ** 2
    )
    scale = 0.25 * grid * math.sqrt(grid) / (grid * grid * grid)
    kernel = jnp.where(square > 0, scale / jnp.maximum(square, 1.0), 0.0)
    selected = jnp.take(orbitals, local_pick[0], axis=0)
    grid_shape = selected.shape[1:]
    total = jnp.zeros_like(selected)
    for step in range(owners.shape[0]):
        sent = spread(orbitals, "band", owners[step])
        density = (sent[:, None] * selected[None]).reshape((-1,) + grid_shape)
        potentials = transform(density, cosine, sine, kernel)
        shaped = potentials.reshape((sent.shape[0], selected.shape[0]) + grid_shape)
        total = total + jnp.sum(shaped * sent[:, None], axis=0)
    return total


def host_tables(grid):
    index = np.arange(grid)
    angle = 2.0 * np.pi * (np.outer(index, index) % grid) / grid
    return np.cos(angle), np.sin(angle)


def as_pair(table):
    high = table.astype(ml_dtypes.bfloat16)
    low = (table - high.astype(np.float64)).astype(ml_dtypes.bfloat16)
    return jnp.asarray(high), jnp.asarray(low)


def blocks(a, b, c, d):
    return np.block([[a, b], [c, d]])


def plane_order(core, half, part):
    base = np.arange(half).reshape(2, -1, part)
    if core:
        base = base[::-1]
    return core * half + base.transpose(1, 0, 2).reshape(-1)


def tables(grid, part):
    cos, sin = host_tables(grid)
    half = grid // 2
    columns = [np.arange(grid), np.concatenate([np.arange(half, grid), np.arange(half)])]
    slabs = [plane_order(core, half, part) for core in range(2)]
    depths = [np.concatenate([slabs[core], slabs[1 - core]]) for core in range(2)]

    def to_spectrum(order):
        c, s = cos[order], sin[order]
        return blocks(c, s, -s, c)

    def from_planes(order):
        c, s = cos[:, order], sin[:, order]
        return blocks(c, s, -s, c)

    def to_planes(order):
        c, s = cos[order], sin[order]
        return blocks(c, -s, s, c)

    def from_spectrum(order):
        c, s = cos[:, order], sin[:, order]
        return blocks(c, -s, s, c)

    both = dict(
        last_fwd=blocks(cos, -sin, sin, cos),
        last_inv=blocks(cos, sin, -sin, cos),
        mid_fwd=np.stack([to_spectrum(order) for order in columns]),
        mid_inv=np.stack([from_spectrum(order) for order in columns]),
        first_fwd=np.stack([from_planes(order) for order in depths]),
        first_inv=np.stack([to_planes(order) for order in depths]),
    )
    return {name: as_pair(value) for name, value in both.items()}


def split(value):
    high = value.astype(BF16)
    return high, (value - high.astype(F32)).astype(BF16)


def mm(a, b):
    return jnp.dot(a, b, preferred_element_type=F32)


def right(data, high, low):
    top, rest = split(data)
    return mm(top, high) + (mm(rest, high) + mm(top, low))


def left(high, low, data):
    top, rest = split(data)
    return mm(high, top) + (mm(high, rest) + mm(low, top))


def pick_body(info, *refs):
    inputs, out, sem = refs[:-2], refs[-2], refs[-1]
    for index, ref in enumerate(inputs):

        @pl.when(info[1] == index)
        def _(ref=ref):
            pltpu.make_async_copy(ref, out, sem).start()

    pltpu.make_async_copy(inputs[0], out, sem).wait()


def forward_body(info, phi, own, other, wyh, wyl, wxh, wxl, keep, send):
    grid = phi.shape[-1]
    half = grid // 2
    part = phi.shape[1]
    rows = 2 * part
    core = info[0]
    near, far = phi[core], phi[1 - core]
    re = jnp.concatenate([near * own[0, 0], far * other[0, 0]], axis=0)
    im = jnp.concatenate([near * own[0, 1], far * other[0, 1]], axis=0)
    data = jnp.concatenate([re, im], axis=-1).reshape(rows * grid, 2 * grid)
    lines = right(data, wyh[...], wyl[...])
    for first in range(0, rows, 2):
        planes = []
        for z in (first, first + 1):
            plane = lines[z * grid : (z + 1) * grid]
            planes.append(jnp.concatenate([plane[:, :grid], plane[:, grid:]], axis=0))
        out = left(wxh[0], wxl[0], jnp.concatenate(planes, axis=1))
        for pos, z in enumerate((first, first + 1)):
            plane = out[:, pos * grid : (pos + 1) * grid]
            for comp in range(2):
                base = comp * grid
                keep[comp, :, z, :] = plane[base : base + half]
                send[comp, :, z, :] = plane[base + half : base + grid]


def middle_body(info, *refs):
    count = (len(refs) - 4) // 4
    keeps, recvs = refs[:count], refs[count : 2 * count]
    wfh, wfl, wih, wil = refs[2 * count : 2 * count + 4]
    keep_outs, send_outs = refs[2 * count + 4 : 3 * count + 4], refs[3 * count + 4 :]
    rows = keeps[0].shape[1]
    grid = keeps[0].shape[-1]
    half = grid // 2
    scale = 0.25 * grid * math.sqrt(grid) / (grid * grid * grid)
    kz = lax.broadcasted_iota(jnp.int32, (grid, grid), 0)
    ky = lax.broadcasted_iota(jnp.int32, (grid, grid), 1)
    fz = jnp.where(kz < grid // 2, kz, kz - grid)
    fy = jnp.where(ky < grid // 2, ky, ky - grid)
    plane_square = fz * fz + fy * fy
    start = info[0] * half + pl.program_id(0) * rows
    lane = lax.broadcasted_iota(jnp.int32, (1, grid), 1)
    for first in range(0, rows, 2):
        planes = []
        for k in (first, first + 1):
            for comp in range(2):
                pieces = [ref[comp, k] for ref in keeps + recvs]
                if k == 0:
                    drop = jnp.where((lane == 0) & (start == 0), pieces[0][0:1], 0.0)
                    pieces = [piece - drop for piece in pieces]
                planes.append(jnp.concatenate(pieces, axis=0))
        data = jnp.concatenate(
            [
                jnp.concatenate(planes[:2], axis=0),
                jnp.concatenate(planes[2:], axis=0),
            ],
            axis=1,
        )
        spec = left(wfh[0], wfl[0], data)
        factors = []
        for k in (first, first + 1):
            kx = start + k
            fx = jnp.where(kx < grid // 2, kx, kx - grid)
            square = (plane_square + fx * fx).astype(F32)
            factors.append(jnp.where(square > 0, scale / jnp.maximum(square, 1.0), 0.0))
        factor = jnp.concatenate(factors, axis=1)
        spec = spec * jnp.concatenate([factor, factor], axis=0)
        out = left(wih[0], wil[0], spec)
        for pos, k in enumerate((first, first + 1)):
            plane = out[:, pos * grid : (pos + 1) * grid]
            for comp in range(2):
                row = comp * grid
                for ref in keep_outs + send_outs:
                    size = ref.shape[2]
                    ref[comp, k] = plane[row : row + size]
                    row += size


def backward_body(info, keep, recv, own, other, wxh, wxl, wyh, wyl, out):
    grid = keep.shape[-1]
    rows = keep.shape[2]
    part = rows // 2
    core = info[0]
    lines = []
    for first in range(0, rows, 2):
        planes = []
        for z in (first, first + 1):
            planes.append(
                jnp.concatenate(
                    [keep[0, :, z, :], recv[0, :, z, :], keep[1, :, z, :], recv[1, :, z, :]],
                    axis=0,
                )
            )
        mixed = left(wxh[0], wxl[0], jnp.concatenate(planes, axis=1))
        for pos in range(2):
            plane = mixed[:, pos * grid : (pos + 1) * grid]
            lines.append(jnp.concatenate([plane[:grid], plane[grid:]], axis=1))
    fields = right(jnp.concatenate(lines, axis=0), wyh[...], wyl[...])
    re = fields[:, :grid].reshape(rows, grid, grid)
    im = fields[:, grid:].reshape(rows, grid, grid)
    out[core] = re[:part] * own[0, 0] + im[:part] * own[0, 1]
    out[1 - core] = re[part:] * other[0, 0] + im[part:] * other[0, 1]


def call(body, grid_size, in_specs, out_specs, out_shape):
    return pl.pallas_call(
        body,
        grid_spec=pltpu.PrefetchScalarGridSpec(
            num_scalar_prefetch=1,
            grid=(grid_size,),
            in_specs=in_specs,
            out_specs=out_specs,
        ),
        out_shape=out_shape,
        compiler_params=pltpu.CompilerParams(vmem_limit_bytes=16 * 1024 * 1024),
    )


def paired(orbitals, owners, local_pick):
    n_orb, half, grid, _ = orbitals.shape
    bands = lax.axis_size("band")
    chips = bands // 2
    layers = chips // 2
    band = lax.axis_index("band")
    x = lax.axis_index("fft")
    core = band % 2
    chip = band // 2
    y = chip % 2
    home = core == x
    axes = ("band", "fft")

    def at(chip_, core_, x_):
        return (chip_ * 2 + core_) * 2 + x_

    def move(value, pairs):
        return lax.ppermute(value, axes, pairs)

    spots = [(t, c, p) for t in range(chips) for c in range(2) for p in range(2)]
    cross = [(at(t, c, p), at(t, p, c)) for t, c, p in spots if c != p]
    sibling = [(at(t, c, p), at(t, 1 - c, p)) for t, c, p in spots]
    over_x = [(at(t, c, p), at(t, c, 1 - p)) for t, c, p in spots]
    over_y = [(at(t, c, p), at(t ^ 1, c, p)) for t, c, p in spots]
    cycle = [2 * z for z in range(layers)] + [2 * z + 1 for z in reversed(range(layers))]
    length = len(cycle)
    after = {cycle[i]: cycle[(i + 1) % length] for i in range(length)}
    before = {chip_: source for source, chip_ in after.items()}
    around = [
        (at(t, c, p), at((after if c == 0 else before)[t], c, p)) for t, c, p in spots
    ]

    def place(chip_):
        return jnp.where(chip_ % 2 == 0, chip_ // 2, length - 1 - chip_ // 2)

    pick = local_pick[0, 0]
    owner = owners[0]
    own_chip = owner // 2
    own_here = chip == own_chip
    direct = (owner % 2) == core
    ahead = (place(chip) - place(own_chip) + length) % length
    distance = jnp.where(core == 0, ahead, (length - ahead) % length)

    part = half // 2 // CHUNKS
    chunk_shape = (n_orb, part, grid, grid)
    cut = orbitals.reshape((n_orb, 2, half // 2, grid, grid))

    def of_half(which, lo, hi):
        begin = (0, which, lo * part, 0, 0)
        piece = lax.dynamic_slice(cut, begin, (n_orb, 1, (hi - lo) * part, grid, grid))
        return piece.reshape((n_orb, hi - lo, part, grid, grid))

    first_out, own_first, cut, orbitals = lax.optimization_barrier(
        (of_half(1 - core, 0, 1), of_half(core, 0, 1), cut, orbitals)
    )
    first_in = move(first_out, sibling)
    chosen_orbital = lax.dynamic_index_in_dim(orbitals, pick, 0, keepdims=False)
    first_in, chosen_orbital, cut = lax.optimization_barrier((first_in, chosen_orbital, cut))
    crossed = move(chosen_orbital, cross)
    bounds = ((1, 3), (3, CHUNKS))
    rest_in = [move(of_half(1 - core, lo, hi), sibling) for lo, hi in bounds]
    fresh = [jnp.where(direct, own_first, first_in)[:, 0]]
    for (lo, hi), other in zip(bounds, rest_in):
        more = jnp.where(direct, of_half(core, lo, hi), other)
        fresh += [more[:, k] for k in range(hi - lo)]
    info = jnp.stack([core.astype(jnp.int32), distance.astype(jnp.int32)])

    steps = CHUNKS + length - 2
    kept = []

    def arrived(k):
        return pl.pallas_call(
            pick_body,
            in_specs=[pl.BlockSpec(memory_space=pltpu.SMEM)]
            + [pl.BlockSpec(memory_space=pl.ANY)] * length,
            out_specs=pl.BlockSpec(memory_space=pltpu.VMEM),
            out_shape=jax.ShapeDtypeStruct(chunk_shape, F32),
            scratch_shapes=[pltpu.SemaphoreType.DMA],
        )(info, *kept[k : k + length])

    carried, phi = None, None
    flying, swapping = [], []
    owns, others = [], []
    t = 0
    while len(others) < CHUNKS:
        joined = [flying.pop(0)] if flying and flying[0][0] <= t else []
        landed = [swapping.pop(0)] if swapping and swapping[0][0] <= t else []
        values = [] if carried is None else [carried]
        values += [item[1] for item in joined + landed]
        if t == 1:
            values.append(info)
        if t == PHI_STEP:
            values.append(crossed)
        if t == PHI_STEP + 1:
            values.append(phi)
        if len(values) > 1:
            values = list(lax.optimization_barrier(tuple(values)))
        if t == 1:
            info = values.pop()
        if t == PHI_STEP + 1:
            phi = values.pop()
        if t == PHI_STEP:
            phi = jnp.where(home, chosen_orbital, values.pop())
        if landed:
            others.append(values.pop())
        if joined:
            mine, got = joined[0][2], values.pop()
            owns.append(jnp.where(home, mine, got))
            swapping.append((t + 1, move(jnp.where(home, got, mine), sibling)))
        carried = None
        if t <= steps:
            held = jnp.where(own_here, fresh[t], values[0]) if 0 < t < CHUNKS else (values or fresh)[0]
            kept.append(held)
            if t < steps:
                carried = move(held, around)
        k = t - length + 1
        if 0 <= k < CHUNKS:
            mine = arrived(k)
            flying.append((t + HOP_STEPS, move(mine, over_x), mine))
        t += 1

    planes = 2 * part
    phi = phi.reshape((2, half // 2, grid, grid))
    own = [jnp.stack(owns[lo:hi]) for lo, hi in GROUPS]
    other = [jnp.stack(others[lo:hi]) for lo, hi in GROUPS]
    table = tables(grid, part)

    def whole(shape):
        return pl.BlockSpec(shape, lambda i, info: (0,) * len(shape))

    def chosen(shape):
        return pl.BlockSpec((1,) + shape, lambda i, info: (info[0],) + (0,) * len(shape))

    square = (2 * grid, 2 * grid)

    pairs = pl.BlockSpec((1,) + chunk_shape, lambda i, info: (i, 0, 0, 0, 0))
    lines = pl.BlockSpec((2, half, planes, grid), lambda i, info: (0, 0, i, 0))
    keeps, sends = [], []
    for g, (lo, hi) in enumerate(GROUPS):
        spectrum = jax.ShapeDtypeStruct((2, half, (hi - lo) * planes, grid), F32)
        slab = pl.BlockSpec((2, part, grid, grid), lambda i, info, lo=lo: (0, lo + i, 0, 0))
        keep, send = call(
            forward_body,
            hi - lo,
            [slab, pairs, pairs] + [whole(square)] * 2 + [chosen(square)] * 2,
            [lines, lines],
            [spectrum, spectrum],
        )(info, phi, own[g], other[g], *table["last_fwd"], *table["mid_fwd"])
        keeps.append(keep)
        sends.append(send)
    recvs = [move(send, sibling) for send in sends]
    cols = [
        pl.BlockSpec((2, ROWS, (hi - lo) * planes, grid), lambda i, info: (0, i, 0, 0))
        for lo, hi in GROUPS
    ]
    shapes = [jax.ShapeDtypeStruct(keep.shape, F32) for keep in keeps]
    results = call(
        middle_body,
        half // ROWS,
        cols * 2 + [chosen(square)] * 4,
        cols * 2,
        shapes * 2,
    )(info, *keeps, *recvs, *table["first_fwd"], *table["first_inv"])
    keeps, sends = results[: len(GROUPS)], results[len(GROUPS) :]
    recvs = [move(send, sibling) for send in sends]
    terms = []
    terms = []
    for lo, hi in TERM_GROUPS:
        g, start = [(g, a) for g, (a, b) in enumerate(GROUPS) if a <= lo < b][0]
        keep, recv = keeps[g], recvs[g]
        if len(terms) > 1:
            there, keep = lax.optimization_barrier((terms[-2][1], keep))
            terms[-2] = (terms[-2][0], there)
        shift = lo - start
        some_lines = pl.BlockSpec(
            (2, half, planes, grid), lambda i, info, shift=shift: (0, 0, shift + i, 0)
        )
        some_pairs = pl.BlockSpec(
            (1,) + chunk_shape, lambda i, info, shift=shift: (shift + i, 0, 0, 0, 0)
        )
        term = call(
            backward_body,
            hi - lo,
            [some_lines, some_lines, some_pairs, some_pairs]
            + [chosen(square)] * 2
            + [whole(square)] * 2,
            pl.BlockSpec((2, part, grid, grid), lambda i, info: (0, i, 0, 0)),
            jax.ShapeDtypeStruct((2, (hi - lo) * part, grid, grid), F32),
        )(info, keep, recv, own[g], other[g], *table["mid_inv"], *table["last_inv"])
        terms.append((term, move(term, cross)))
    total = jnp.concatenate([jnp.where(home, *both) for both in terms], axis=1)
    return total.reshape((1, half, grid, grid))


def solution(mesh):
    in_specs = (P("band", "fft", None, None), P(), P("band", None))
    out_specs = P("band", "fft", None, None)
    two_slabs = mesh.shape["fft"] == 2 and mesh.shape["band"] % 4 == 0

    def on_device(orbitals, owners, local_pick):
        fits = (
            orbitals.shape[0] == 2
            and orbitals.shape[1] == CHUNKS * ROWS
            and orbitals.shape[-1] % 128 == 0
            and owners.shape[0] == 1
            and local_pick.shape == (1, 1)
        )
        if two_slabs and fits:
            return paired(orbitals, owners, local_pick)
        return general(orbitals, owners, local_pick)

    return jax.shard_map(
        on_device, mesh=mesh, in_specs=in_specs, out_specs=out_specs, check_vma=False
    )
```

```python
import functools
import math

import jax
import jax.numpy as jnp
import ml_dtypes
import numpy as np
from jax import lax
from jax.experimental import pallas as pl
from jax.experimental.pallas import tpu as pltpu
from jax.sharding import PartitionSpec as P

F32 = jnp.float32
BF16 = jnp.bfloat16
ROWS = 8
CHUNKS = 8
UNITS = 2
MIDDLE_ROWS = 16
GROUPS = ((0, 4), (4, 6), (6, 8))
TERM_GROUPS = ((0, 2), (2, 4), (4, 6), (6, 8))
HOP_STEPS = 2
PHI_STEP = 6


def spread(shard, axis, root):
    mine = lax.axis_index(axis) == root
    return lax.psum(jnp.where(mine, shard, jnp.zeros_like(shard)), axis)


def dft_tables(size):
    index = jnp.arange(size, dtype=jnp.int32)
    product = index[:, None] * index[None, :] % size
    angle = product.astype(jnp.float32) * (2.0 * math.pi / size)
    return (jnp.cos(angle), jnp.sin(angle))


def signed_freq(index, size):
    return jnp.where(index < size // 2, index, index - size).astype(jnp.float32)


def along(form, data, table):
    return jnp.einsum(form, data, table, precision=lax.Precision.HIGHEST)


def transform(density, cosine, sine, kernel):
    last_form = "pzxy,yk->pzxk"
    middle_form = "pzxy,xk->pzky"
    first_form = "pzab,zk->pkab"
    evens = density[0::2]
    odds = density[1::2]
    real_part = along(last_form, evens, cosine) + along(last_form, odds, sine)
    imag_part = along(last_form, odds, cosine) - along(last_form, evens, sine)
    mixed_real = along(middle_form, real_part, cosine) + along(middle_form, imag_part, sine)
    mixed_imag = along(middle_form, imag_part, cosine) - along(middle_form, real_part, sine)
    line_real = lax.all_to_all(mixed_real, "fft", split_axis=2, concat_axis=1, tiled=True)
    line_imag = lax.all_to_all(mixed_imag, "fft", split_axis=2, concat_axis=1, tiled=True)
    spec_real = along(first_form, line_real, cosine) + along(first_form, line_imag, sine)
    spec_imag = along(first_form, line_imag, cosine) - along(first_form, line_real, sine)
    spec_real = spec_real * kernel
    spec_imag = spec_imag * kernel
    back_real = along(first_form, spec_real, cosine) - along(first_form, spec_imag, sine)
    back_imag = along(first_form, spec_imag, cosine) + along(first_form, spec_real, sine)
    slab_real = lax.all_to_all(back_real, "fft", split_axis=1, concat_axis=2, tiled=True)
    slab_imag = lax.all_to_all(back_imag, "fft", split_axis=1, concat_axis=2, tiled=True)
    inner_real = along(middle_form, slab_real, cosine) - along(middle_form, slab_imag, sine)
    inner_imag = along(middle_form, slab_imag, cosine) + along(middle_form, slab_real, sine)
    first_field = along(last_form, inner_real, cosine) - along(last_form, inner_imag, sine)
    second_field = along(last_form, inner_imag, cosine) + along(last_form, inner_real, sine)
    return jnp.stack([first_field, second_field], 1).reshape(density.shape)


def general(orbitals, owners, local_pick):
    grid = orbitals.shape[-1]
    cosine, sine = dft_tables(grid)
    groups = lax.axis_size("fft")
    width = grid // groups
    start = lax.axis_index("fft") * width
    freq_first = signed_freq(jnp.arange(grid, dtype=jnp.int32), grid)
    freq_second = signed_freq(start + jnp.arange(width, dtype=jnp.int32), grid)
    square = (
        freq_first[:, None, None] ** 2
        + freq_second[None, :, None] ** 2
        + freq_first[None, None, :] ** 2
    )
    scale = 0.25 * grid * math.sqrt(grid) / (grid * grid * grid)
    kernel = jnp.where(square > 0, scale / jnp.maximum(square, 1.0), 0.0)
    selected = jnp.take(orbitals, local_pick[0], axis=0)
    grid_shape = selected.shape[1:]
    total = jnp.zeros_like(selected)
    for step in range(owners.shape[0]):
        sent = spread(orbitals, "band", owners[step])
        density = (sent[:, None] * selected[None]).reshape((-1,) + grid_shape)
        potentials = transform(density, cosine, sine, kernel)
        shaped = potentials.reshape((sent.shape[0], selected.shape[0]) + grid_shape)
        total = total + jnp.sum(shaped * sent[:, None], axis=0)
    return total


def host_tables(grid):
    index = np.arange(grid)
    angle = 2.0 * np.pi * (np.outer(index, index) % grid) / grid
    return np.cos(angle), np.sin(angle)


def as_pair(table):
    high = table.astype(ml_dtypes.bfloat16)
    low = (table - high.astype(np.float64)).astype(ml_dtypes.bfloat16)
    return jnp.asarray(high), jnp.asarray(low)


def blocks(a, b, c, d):
    return np.block([[a, b], [c, d]])


def plane_order(core, half, part):
    base = np.arange(half).reshape(2, -1, part)
    if core:
        base = base[::-1]
    return core * half + base.transpose(1, 0, 2).reshape(-1)


def tables(grid, part):
    cos, sin = host_tables(grid)
    half = grid // 2
    columns = [np.arange(grid), np.concatenate([np.arange(half, grid), np.arange(half)])]
    slabs = [plane_order(core, half, part) for core in range(2)]
    depths = [np.concatenate([slabs[core], slabs[1 - core]]) for core in range(2)]

    def to_spectrum(order):
        c, s = cos[order], sin[order]
        return blocks(c, s, -s, c)

    def from_planes(order):
        c, s = cos[:, order], sin[:, order]
        return blocks(c, s, -s, c)

    def to_planes(order):
        c, s = cos[order], sin[order]
        return blocks(c, -s, s, c)

    def from_spectrum(order):
        c, s = cos[:, order], sin[:, order]
        return blocks(c, -s, s, c)

    both = dict(
        last_fwd=blocks(cos, -sin, sin, cos),
        last_inv=blocks(cos, sin, -sin, cos),
        mid_fwd=np.stack([to_spectrum(order) for order in columns]),
        mid_inv=np.stack([from_spectrum(order) for order in columns]),
        first_fwd=np.stack([from_planes(order) for order in depths]),
        first_inv=np.stack([to_planes(order) for order in depths]),
    )
    return {name: as_pair(value) for name, value in both.items()}


def split(value):
    high = value.astype(BF16)
    return high, (value - high.astype(F32)).astype(BF16)


def mm(a, b):
    return jnp.dot(a, b, preferred_element_type=F32)


def right(data, high, low):
    top, rest = split(data)
    return mm(top, high) + (mm(rest, high) + mm(top, low))


def left(high, low, data):
    top, rest = split(data)
    return mm(high, top) + (mm(high, rest) + mm(low, top))


def pick_body(info, *refs):
    inputs, out, sem = refs[:-2], refs[-2], refs[-1]
    for index, ref in enumerate(inputs):

        @pl.when(info[1] == index)
        def _(ref=ref):
            pltpu.make_async_copy(ref, out, sem).start()

    pltpu.make_async_copy(inputs[0], out, sem).wait()


def forward_body(info, phi, own, other, wyh, wyl, wxh, wxl, keep, send):
    grid = phi.shape[-1]
    half = grid // 2
    part = phi.shape[1]
    rows = 2 * part
    core = info[0]
    units = own.shape[0]
    part = part // units
    re, im = [], []
    for u in range(units):
        near = phi[core, u * part : (u + 1) * part]
        far = phi[1 - core, u * part : (u + 1) * part]
        re += [near * own[u, 0], far * other[u, 0]]
        im += [near * own[u, 1], far * other[u, 1]]
    re = jnp.concatenate(re, axis=0)
    im = jnp.concatenate(im, axis=0)
    data = jnp.concatenate([re, im], axis=-1).reshape(rows * grid, 2 * grid)
    lines = right(data, wyh[...], wyl[...])
    for first in range(0, rows, 2):
        planes = []
        for z in (first, first + 1):
            plane = lines[z * grid : (z + 1) * grid]
            planes.append(jnp.concatenate([plane[:, :grid], plane[:, grid:]], axis=0))
        out = left(wxh[0], wxl[0], jnp.concatenate(planes, axis=1))
        for pos, z in enumerate((first, first + 1)):
            plane = out[:, pos * grid : (pos + 1) * grid]
            for comp in range(2):
                base = comp * grid
                keep[comp, :, z, :] = plane[base : base + half]
                send[comp, :, z, :] = plane[base + half : base + grid]


def middle_body(info, *refs):
    count = (len(refs) - 4) // 4
    keeps, recvs = refs[:count], refs[count : 2 * count]
    wfh, wfl, wih, wil = refs[2 * count : 2 * count + 4]
    keep_outs, send_outs = refs[2 * count + 4 : 3 * count + 4], refs[3 * count + 4 :]
    rows = keeps[0].shape[1]
    grid = keeps[0].shape[-1]
    half = grid // 2
    scale = 0.25 * grid * math.sqrt(grid) / (grid * grid * grid)
    kz = lax.broadcasted_iota(jnp.int32, (grid, grid), 0)
    ky = lax.broadcasted_iota(jnp.int32, (grid, grid), 1)
    fz = jnp.where(kz < grid // 2, kz, kz - grid)
    fy = jnp.where(ky < grid // 2, ky, ky - grid)
    plane_square = fz * fz + fy * fy
    start = info[0] * half + pl.program_id(0) * rows
    lane = lax.broadcasted_iota(jnp.int32, (1, grid), 1)
    for first in range(0, rows, 2):
        planes = []
        for k in (first, first + 1):
            for comp in range(2):
                pieces = [ref[comp, k] for ref in keeps + recvs]
                if k == 0:
                    drop = jnp.where((lane == 0) & (start == 0), pieces[0][0:1], 0.0)
                    pieces = [piece - drop for piece in pieces]
                planes.append(jnp.concatenate(pieces, axis=0))
        data = jnp.concatenate(
            [
                jnp.concatenate(planes[:2], axis=0),
                jnp.concatenate(planes[2:], axis=0),
            ],
            axis=1,
        )
        spec = left(wfh[0], wfl[0], data)
        factors = []
        for k in (first, first + 1):
            kx = start + k
            fx = jnp.where(kx < grid // 2, kx, kx - grid)
            square = (plane_square + fx * fx).astype(F32)
            factors.append(jnp.where(square > 0, scale / jnp.maximum(square, 1.0), 0.0))
        factor = jnp.concatenate(factors, axis=1)
        spec = spec * jnp.concatenate([factor, factor], axis=0)
        out = left(wih[0], wil[0], spec)
        for pos, k in enumerate((first, first + 1)):
            plane = out[:, pos * grid : (pos + 1) * grid]
            for comp in range(2):
                row = comp * grid
                for ref in keep_outs + send_outs:
                    size = ref.shape[2]
                    ref[comp, k] = plane[row : row + size]
                    row += size


def backward_body(info, keep, recv, own, other, wxh, wxl, wyh, wyl, out):
    grid = keep.shape[-1]
    rows = keep.shape[2]
    units = own.shape[0]
    part = rows // 2 // units
    core = info[0]
    lines = []
    for first in range(0, rows, 2):
        planes = []
        for z in (first, first + 1):
            planes.append(
                jnp.concatenate(
                    [keep[0, :, z, :], recv[0, :, z, :], keep[1, :, z, :], recv[1, :, z, :]],
                    axis=0,
                )
            )
        mixed = left(wxh[0], wxl[0], jnp.concatenate(planes, axis=1))
        for pos in range(2):
            plane = mixed[:, pos * grid : (pos + 1) * grid]
            lines.append(jnp.concatenate([plane[:grid], plane[grid:]], axis=1))
    fields = right(jnp.concatenate(lines, axis=0), wyh[...], wyl[...])
    re = fields[:, :grid].reshape(rows, grid, grid)
    im = fields[:, grid:].reshape(rows, grid, grid)
    for u in range(units):
        near = slice(2 * u * part, (2 * u + 1) * part)
        far = slice((2 * u + 1) * part, (2 * u + 2) * part)
        place = pl.ds(u * part, part)
        out[core, place] = re[near] * own[u, 0] + im[near] * own[u, 1]
        out[1 - core, place] = re[far] * other[u, 0] + im[far] * other[u, 1]


def call(body, grid_size, in_specs, out_specs, out_shape):
    return pl.pallas_call(
        body,
        grid_spec=pltpu.PrefetchScalarGridSpec(
            num_scalar_prefetch=1,
            grid=(grid_size,),
            in_specs=in_specs,
            out_specs=out_specs,
        ),
        out_shape=out_shape,
        compiler_params=pltpu.CompilerParams(vmem_limit_bytes=32 * 1024 * 1024),
    )


def paired(orbitals, owners, local_pick):
    n_orb, half, grid, _ = orbitals.shape
    bands = lax.axis_size("band")
    chips = bands // 2
    layers = chips // 2
    band = lax.axis_index("band")
    x = lax.axis_index("fft")
    core = band % 2
    chip = band // 2
    y = chip % 2
    home = core == x
    axes = ("band", "fft")

    def at(chip_, core_, x_):
        return (chip_ * 2 + core_) * 2 + x_

    def move(value, pairs):
        return lax.ppermute(value, axes, pairs)

    spots = [(t, c, p) for t in range(chips) for c in range(2) for p in range(2)]
    cross = [(at(t, c, p), at(t, p, c)) for t, c, p in spots if c != p]
    sibling = [(at(t, c, p), at(t, 1 - c, p)) for t, c, p in spots]
    over_x = [(at(t, c, p), at(t, c, 1 - p)) for t, c, p in spots]
    over_y = [(at(t, c, p), at(t ^ 1, c, p)) for t, c, p in spots]
    cycle = [2 * z for z in range(layers)] + [2 * z + 1 for z in reversed(range(layers))]
    length = len(cycle)
    after = {cycle[i]: cycle[(i + 1) % length] for i in range(length)}
    before = {chip_: source for source, chip_ in after.items()}
    around = [
        (at(t, c, p), at((after if c == 0 else before)[t], c, p)) for t, c, p in spots
    ]

    def place(chip_):
        return jnp.where(chip_ % 2 == 0, chip_ // 2, length - 1 - chip_ // 2)

    pick = local_pick[0, 0]
    owner = owners[0]
    own_chip = owner // 2
    own_here = chip == own_chip
    direct = (owner % 2) == core
    ahead = (place(chip) - place(own_chip) + length) % length
    distance = jnp.where(core == 0, ahead, (length - ahead) % length)

    part = half // 2 // CHUNKS
    chunk_shape = (n_orb, part, grid, grid)
    cut = orbitals.reshape((n_orb, 2, half // 2, grid, grid))

    def of_half(which, lo, hi):
        begin = (0, which, lo * part, 0, 0)
        piece = lax.dynamic_slice(cut, begin, (n_orb, 1, (hi - lo) * part, grid, grid))
        return piece.reshape((n_orb, hi - lo, part, grid, grid))

    first_out, own_first, cut, orbitals = lax.optimization_barrier(
        (of_half(1 - core, 0, 1), of_half(core, 0, 1), cut, orbitals)
    )
    first_in = move(first_out, sibling)
    chosen_orbital = lax.dynamic_index_in_dim(orbitals, pick, 0, keepdims=False)
    rest_in = move(orbitals, sibling).reshape(cut.shape)
    first_in, chosen_orbital, cut = lax.optimization_barrier((first_in, chosen_orbital, cut))
    crossed = move(chosen_orbital, cross)
    fresh = [jnp.where(direct, own_first, first_in)[:, 0]]
    for k in range(1, CHUNKS):
        begin = (0, core, k * part, 0, 0)
        size = (n_orb, 1, part, grid, grid)
        both = [lax.dynamic_slice(v, begin, size)[:, 0] for v in (cut, rest_in)]
        fresh.append(jnp.where(direct, *both))
    info = jnp.stack([core.astype(jnp.int32), distance.astype(jnp.int32)])

    steps = CHUNKS + length - 2
    kept = []

    def arrived(k):
        return pl.pallas_call(
            pick_body,
            in_specs=[pl.BlockSpec(memory_space=pltpu.SMEM)]
            + [pl.BlockSpec(memory_space=pl.ANY)] * length,
            out_specs=pl.BlockSpec(memory_space=pltpu.VMEM),
            out_shape=jax.ShapeDtypeStruct(chunk_shape, F32),
            scratch_shapes=[pltpu.SemaphoreType.DMA],
        )(info, *kept[k : k + length])

    carried, phi = None, None
    flying, swapping = [], []
    owns, others = [], []
    t = 0
    while len(others) < CHUNKS:
        joined = [flying.pop(0)] if flying and flying[0][0] <= t else []
        landed = [swapping.pop(0)] if swapping and swapping[0][0] <= t else []
        values = [] if carried is None else [carried]
        values += [item[1] for item in joined + landed]
        if t == 1:
            values.append(info)
        if t == 2:
            values += fresh[3:]
        if t == PHI_STEP:
            values.append(crossed)
        if t == PHI_STEP + 1:
            values.append(phi)
        if len(values) > 1:
            values = list(lax.optimization_barrier(tuple(values)))
        if t == 2:
            fresh[3:] = values[-len(fresh[3:]) :]
            values = values[: -len(fresh[3:])]
        if t == 1:
            info = values.pop()
        if t == PHI_STEP + 1:
            phi = values.pop()
        if t == PHI_STEP:
            phi = jnp.where(home, chosen_orbital, values.pop())
        if landed:
            others.append(values.pop())
        if joined:
            mine, got = joined[0][2], values.pop()
            owns.append(jnp.where(home, mine, got))
            swapping.append((t + 1, move(jnp.where(home, got, mine), sibling)))
        carried = None
        if t <= steps:
            held = jnp.where(own_here, fresh[t], values[0]) if 0 < t < CHUNKS else (values or fresh)[0]
            kept.append(held)
            if t < steps:
                carried = move(held, around)
        k = t - length + 1
        if 0 <= k < CHUNKS:
            mine = arrived(k)
            flying.append((t + HOP_STEPS, move(mine, over_x), mine))
        t += 1

    planes = 2 * part
    phi = phi.reshape((2, half // 2, grid, grid))
    own = [jnp.stack(owns[lo:hi]) for lo, hi in GROUPS]
    other = [jnp.stack(others[lo:hi]) for lo, hi in GROUPS]
    table = tables(grid, part)

    def whole(shape):
        return pl.BlockSpec(shape, lambda i, info: (0,) * len(shape))

    def chosen(shape):
        return pl.BlockSpec((1,) + shape, lambda i, info: (info[0],) + (0,) * len(shape))

    square = (2 * grid, 2 * grid)

    pairs = pl.BlockSpec((UNITS,) + chunk_shape, lambda i, info: (i, 0, 0, 0, 0))
    lines = pl.BlockSpec((2, half, UNITS * planes, grid), lambda i, info: (0, 0, i, 0))
    keeps, sends = [], []
    for g, (lo, hi) in enumerate(GROUPS):
        spectrum = jax.ShapeDtypeStruct((2, half, (hi - lo) * planes, grid), F32)
        slab = pl.BlockSpec(
            (2, UNITS * part, grid, grid), lambda i, info, lo=lo: (0, lo // UNITS + i, 0, 0)
        )
        keep, send = call(
            forward_body,
            (hi - lo) // UNITS,
            [slab, pairs, pairs] + [whole(square)] * 2 + [chosen(square)] * 2,
            [lines, lines],
            [spectrum, spectrum],
        )(info, phi, own[g], other[g], *table["last_fwd"], *table["mid_fwd"])
        keeps.append(keep)
        sends.append(send)
    recvs = [move(send, sibling) for send in sends]
    cols = [
        pl.BlockSpec((2, MIDDLE_ROWS, (hi - lo) * planes, grid), lambda i, info: (0, i, 0, 0))
        for lo, hi in GROUPS
    ]
    shapes = [jax.ShapeDtypeStruct(keep.shape, F32) for keep in keeps]
    results = call(
        middle_body,
        half // MIDDLE_ROWS,
        cols * 2 + [chosen(square)] * 4,
        cols * 2,
        shapes * 2,
    )(info, *keeps, *recvs, *table["first_fwd"], *table["first_inv"])
    keeps, sends = results[: len(GROUPS)], results[len(GROUPS) :]
    recvs = [move(send, sibling) for send in sends]
    terms = []
    terms = []
    for lo, hi in TERM_GROUPS:
        g, start = [(g, a) for g, (a, b) in enumerate(GROUPS) if a <= lo < b][0]
        keep, recv = keeps[g], recvs[g]
        if len(terms) > 1:
            there, keep = lax.optimization_barrier((terms[-2][1], keep))
            terms[-2] = (terms[-2][0], there)
        shift = (lo - start) // UNITS
        some_lines = pl.BlockSpec(
            (2, half, UNITS * planes, grid), lambda i, info, shift=shift: (0, 0, shift + i, 0)
        )
        some_pairs = pl.BlockSpec(
            (UNITS,) + chunk_shape, lambda i, info, shift=shift: (shift + i, 0, 0, 0, 0)
        )
        term = call(
            backward_body,
            (hi - lo) // UNITS,
            [some_lines, some_lines, some_pairs, some_pairs]
            + [chosen(square)] * 2
            + [whole(square)] * 2,
            pl.BlockSpec((2, UNITS * part, grid, grid), lambda i, info: (0, i, 0, 0)),
            jax.ShapeDtypeStruct((2, (hi - lo) * part, grid, grid), F32),
        )(info, keep, recv, own[g], other[g], *table["mid_inv"], *table["last_inv"])
        terms.append((term, move(term, cross)))
    total = jnp.concatenate([jnp.where(home, *both) for both in terms], axis=1)
    return total.reshape((1, half, grid, grid))


def solution(mesh):
    in_specs = (P("band", "fft", None, None), P(), P("band", None))
    out_specs = P("band", "fft", None, None)
    two_slabs = mesh.shape["fft"] == 2 and mesh.shape["band"] % 4 == 0

    def on_device(orbitals, owners, local_pick):
        fits = (
            orbitals.shape[0] == 2
            and orbitals.shape[1] == CHUNKS * ROWS
            and orbitals.shape[-1] % 128 == 0
            and owners.shape[0] == 1
            and local_pick.shape == (1, 1)
        )
        if two_slabs and fits:
            return paired(orbitals, owners, local_pick)
        return general(orbitals, owners, local_pick)

    return jax.shard_map(
        on_device, mesh=mesh, in_specs=in_specs, out_specs=out_specs, check_vma=False
    )
```

```python
import functools
import math

import jax
import jax.numpy as jnp
import ml_dtypes
import numpy as np
from jax import lax
from jax.experimental import pallas as pl
from jax.experimental.pallas import tpu as pltpu
from jax.sharding import PartitionSpec as P

F32 = jnp.float32
BF16 = jnp.bfloat16
ROWS = 8
CHUNKS = 8
UNITS = 2
MIDDLE_ROWS = 32
GROUPS = ((0, 4), (4, 6), (6, 8))
TERM_GROUPS = ((0, 2), (2, 4), (4, 6), (6, 8))
HOP_STEPS = 2
PHI_STEP = 6


def spread(shard, axis, root):
    mine = lax.axis_index(axis) == root
    return lax.psum(jnp.where(mine, shard, jnp.zeros_like(shard)), axis)


def dft_tables(size):
    index = jnp.arange(size, dtype=jnp.int32)
    product = index[:, None] * index[None, :] % size
    angle = product.astype(jnp.float32) * (2.0 * math.pi / size)
    return (jnp.cos(angle), jnp.sin(angle))


def signed_freq(index, size):
    return jnp.where(index < size // 2, index, index - size).astype(jnp.float32)


def along(form, data, table):
    return jnp.einsum(form, data, table, precision=lax.Precision.HIGHEST)


def transform(density, cosine, sine, kernel):
    last_form = "pzxy,yk->pzxk"
    middle_form = "pzxy,xk->pzky"
    first_form = "pzab,zk->pkab"
    evens = density[0::2]
    odds = density[1::2]
    real_part = along(last_form, evens, cosine) + along(last_form, odds, sine)
    imag_part = along(last_form, odds, cosine) - along(last_form, evens, sine)
    mixed_real = along(middle_form, real_part, cosine) + along(middle_form, imag_part, sine)
    mixed_imag = along(middle_form, imag_part, cosine) - along(middle_form, real_part, sine)
    line_real = lax.all_to_all(mixed_real, "fft", split_axis=2, concat_axis=1, tiled=True)
    line_imag = lax.all_to_all(mixed_imag, "fft", split_axis=2, concat_axis=1, tiled=True)
    spec_real = along(first_form, line_real, cosine) + along(first_form, line_imag, sine)
    spec_imag = along(first_form, line_imag, cosine) - along(first_form, line_real, sine)
    spec_real = spec_real * kernel
    spec_imag = spec_imag * kernel
    back_real = along(first_form, spec_real, cosine) - along(first_form, spec_imag, sine)
    back_imag = along(first_form, spec_imag, cosine) + along(first_form, spec_real, sine)
    slab_real = lax.all_to_all(back_real, "fft", split_axis=1, concat_axis=2, tiled=True)
    slab_imag = lax.all_to_all(back_imag, "fft", split_axis=1, concat_axis=2, tiled=True)
    inner_real = along(middle_form, slab_real, cosine) - along(middle_form, slab_imag, sine)
    inner_imag = along(middle_form, slab_imag, cosine) + along(middle_form, slab_real, sine)
    first_field = along(last_form, inner_real, cosine) - along(last_form, inner_imag, sine)
    second_field = along(last_form, inner_imag, cosine) + along(last_form, inner_real, sine)
    return jnp.stack([first_field, second_field], 1).reshape(density.shape)


def general(orbitals, owners, local_pick):
    grid = orbitals.shape[-1]
    cosine, sine = dft_tables(grid)
    groups = lax.axis_size("fft")
    width = grid // groups
    start = lax.axis_index("fft") * width
    freq_first = signed_freq(jnp.arange(grid, dtype=jnp.int32), grid)
    freq_second = signed_freq(start + jnp.arange(width, dtype=jnp.int32), grid)
    square = (
        freq_first[:, None, None] ** 2
        + freq_second[None, :, None] ** 2
        + freq_first[None, None, :] ** 2
    )
    scale = 0.25 * grid * math.sqrt(grid) / (grid * grid * grid)
    kernel = jnp.where(square > 0, scale / jnp.maximum(square, 1.0), 0.0)
    selected = jnp.take(orbitals, local_pick[0], axis=0)
    grid_shape = selected.shape[1:]
    total = jnp.zeros_like(selected)
    for step in range(owners.shape[0]):
        sent = spread(orbitals, "band", owners[step])
        density = (sent[:, None] * selected[None]).reshape((-1,) + grid_shape)
        potentials = transform(density, cosine, sine, kernel)
        shaped = potentials.reshape((sent.shape[0], selected.shape[0]) + grid_shape)
        total = total + jnp.sum(shaped * sent[:, None], axis=0)
    return total


def host_tables(grid):
    index = np.arange(grid)
    angle = 2.0 * np.pi * (np.outer(index, index) % grid) / grid
    return np.cos(angle), np.sin(angle)


def as_pair(table):
    high = table.astype(ml_dtypes.bfloat16)
    low = (table - high.astype(np.float64)).astype(ml_dtypes.bfloat16)
    return jnp.asarray(high), jnp.asarray(low)


def blocks(a, b, c, d):
    return np.block([[a, b], [c, d]])


def plane_order(core, half, part):
    base = np.arange(half).reshape(2, -1, part)
    if core:
        base = base[::-1]
    return core * half + base.transpose(1, 0, 2).reshape(-1)


def tables(grid, part):
    cos, sin = host_tables(grid)
    half = grid // 2
    columns = [np.arange(grid), np.concatenate([np.arange(half, grid), np.arange(half)])]
    slabs = [plane_order(core, half, part) for core in range(2)]
    depths = [np.concatenate([slabs[core], slabs[1 - core]]) for core in range(2)]

    def to_spectrum(order):
        c, s = cos[order], sin[order]
        return blocks(c, s, -s, c)

    def from_planes(order):
        c, s = cos[:, order], sin[:, order]
        return blocks(c, s, -s, c)

    def to_planes(order):
        c, s = cos[order], sin[order]
        return blocks(c, -s, s, c)

    def from_spectrum(order):
        c, s = cos[:, order], sin[:, order]
        return blocks(c, -s, s, c)

    both = dict(
        last_fwd=blocks(cos, -sin, sin, cos),
        last_inv=blocks(cos, sin, -sin, cos),
        mid_fwd=np.stack([to_spectrum(order) for order in columns]),
        mid_inv=np.stack([from_spectrum(order) for order in columns]),
        first_fwd=np.stack([from_planes(order) for order in depths]),
        first_inv=np.stack([to_planes(order) for order in depths]),
    )
    return {name: as_pair(value) for name, value in both.items()}


def split(value):
    high = value.astype(BF16)
    return high, (value - high.astype(F32)).astype(BF16)


def mm(a, b):
    return jnp.dot(a, b, preferred_element_type=F32)


def right(data, high, low):
    top, rest = split(data)
    return mm(top, high) + (mm(rest, high) + mm(top, low))


def left(high, low, data):
    top, rest = split(data)
    return mm(high, top) + (mm(high, rest) + mm(low, top))


def pick_body(info, *refs):
    inputs, out, sem = refs[:-2], refs[-2], refs[-1]
    for index, ref in enumerate(inputs):

        @pl.when(info[1] == index)
        def _(ref=ref):
            pltpu.make_async_copy(ref, out, sem).start()

    pltpu.make_async_copy(inputs[0], out, sem).wait()


def forward_body(info, phi, own, other, wyh, wyl, wxh, wxl, keep, send):
    grid = phi.shape[-1]
    half = grid // 2
    part = phi.shape[1]
    rows = 2 * part
    core = info[0]
    units = own.shape[0]
    part = part // units
    re, im = [], []
    for u in range(units):
        near = phi[core, u * part : (u + 1) * part]
        far = phi[1 - core, u * part : (u + 1) * part]
        re += [near * own[u, 0], far * other[u, 0]]
        im += [near * own[u, 1], far * other[u, 1]]
    re = jnp.concatenate(re, axis=0)
    im = jnp.concatenate(im, axis=0)
    data = jnp.concatenate([re, im], axis=-1).reshape(rows * grid, 2 * grid)
    lines = right(data, wyh[...], wyl[...])
    for first in range(0, rows, 2):
        planes = []
        for z in (first, first + 1):
            plane = lines[z * grid : (z + 1) * grid]
            planes.append(jnp.concatenate([plane[:, :grid], plane[:, grid:]], axis=0))
        out = left(wxh[0], wxl[0], jnp.concatenate(planes, axis=1))
        for pos, z in enumerate((first, first + 1)):
            plane = out[:, pos * grid : (pos + 1) * grid]
            for comp in range(2):
                base = comp * grid
                keep[comp, :, z, :] = plane[base : base + half]
                send[comp, :, z, :] = plane[base + half : base + grid]


def middle_body(info, *refs):
    count = (len(refs) - 4) // 4
    keeps, recvs = refs[:count], refs[count : 2 * count]
    wfh, wfl, wih, wil = refs[2 * count : 2 * count + 4]
    keep_outs, send_outs = refs[2 * count + 4 : 3 * count + 4], refs[3 * count + 4 :]
    rows = keeps[0].shape[1]
    grid = keeps[0].shape[-1]
    half = grid // 2
    scale = 0.25 * grid * math.sqrt(grid) / (grid * grid * grid)
    kz = lax.broadcasted_iota(jnp.int32, (grid, grid), 0)
    ky = lax.broadcasted_iota(jnp.int32, (grid, grid), 1)
    fz = jnp.where(kz < grid // 2, kz, kz - grid)
    fy = jnp.where(ky < grid // 2, ky, ky - grid)
    plane_square = fz * fz + fy * fy
    start = info[0] * half + pl.program_id(0) * rows
    lane = lax.broadcasted_iota(jnp.int32, (1, grid), 1)
    for first in range(0, rows, 2):
        planes = []
        for k in (first, first + 1):
            for comp in range(2):
                pieces = [ref[comp, k] for ref in keeps + recvs]
                if k == 0:
                    drop = jnp.where((lane == 0) & (start == 0), pieces[0][0:1], 0.0)
                    pieces = [piece - drop for piece in pieces]
                planes.append(jnp.concatenate(pieces, axis=0))
        data = jnp.concatenate(
            [
                jnp.concatenate(planes[:2], axis=0),
                jnp.concatenate(planes[2:], axis=0),
            ],
            axis=1,
        )
        spec = left(wfh[0], wfl[0], data)
        factors = []
        for k in (first, first + 1):
            kx = start + k
            fx = jnp.where(kx < grid // 2, kx, kx - grid)
            square = (plane_square + fx * fx).astype(F32)
            factors.append(jnp.where(square > 0, scale / jnp.maximum(square, 1.0), 0.0))
        factor = jnp.concatenate(factors, axis=1)
        spec = spec * jnp.concatenate([factor, factor], axis=0)
        out = left(wih[0], wil[0], spec)
        for pos, k in enumerate((first, first + 1)):
            plane = out[:, pos * grid : (pos + 1) * grid]
            for comp in range(2):
                row = comp * grid
                for ref in keep_outs + send_outs:
                    size = ref.shape[2]
                    ref[comp, k] = plane[row : row + size]
                    row += size


def backward_body(info, keep, recv, own, other, wxh, wxl, wyh, wyl, out):
    grid = keep.shape[-1]
    rows = keep.shape[2]
    units = own.shape[0]
    part = rows // 2 // units
    core = info[0]
    lines = []
    for first in range(0, rows, 2):
        planes = []
        for z in (first, first + 1):
            planes.append(
                jnp.concatenate(
                    [keep[0, :, z, :], recv[0, :, z, :], keep[1, :, z, :], recv[1, :, z, :]],
                    axis=0,
                )
            )
        mixed = left(wxh[0], wxl[0], jnp.concatenate(planes, axis=1))
        for pos in range(2):
            plane = mixed[:, pos * grid : (pos + 1) * grid]
            lines.append(jnp.concatenate([plane[:grid], plane[grid:]], axis=1))
    fields = right(jnp.concatenate(lines, axis=0), wyh[...], wyl[...])
    re = fields[:, :grid].reshape(rows, grid, grid)
    im = fields[:, grid:].reshape(rows, grid, grid)
    for u in range(units):
        near = slice(2 * u * part, (2 * u + 1) * part)
        far = slice((2 * u + 1) * part, (2 * u + 2) * part)
        place = pl.ds(u * part, part)
        out[core, place] = re[near] * own[u, 0] + im[near] * own[u, 1]
        out[1 - core, place] = re[far] * other[u, 0] + im[far] * other[u, 1]


def call(body, grid_size, in_specs, out_specs, out_shape):
    return pl.pallas_call(
        body,
        grid_spec=pltpu.PrefetchScalarGridSpec(
            num_scalar_prefetch=1,
            grid=(grid_size,),
            in_specs=in_specs,
            out_specs=out_specs,
        ),
        out_shape=out_shape,
        compiler_params=pltpu.CompilerParams(vmem_limit_bytes=32 * 1024 * 1024),
    )


def paired(orbitals, owners, local_pick):
    n_orb, half, grid, _ = orbitals.shape
    bands = lax.axis_size("band")
    chips = bands // 2
    layers = chips // 2
    band = lax.axis_index("band")
    x = lax.axis_index("fft")
    core = band % 2
    chip = band // 2
    y = chip % 2
    home = core == x
    axes = ("band", "fft")

    def at(chip_, core_, x_):
        return (chip_ * 2 + core_) * 2 + x_

    def move(value, pairs):
        return lax.ppermute(value, axes, pairs)

    spots = [(t, c, p) for t in range(chips) for c in range(2) for p in range(2)]
    cross = [(at(t, c, p), at(t, p, c)) for t, c, p in spots if c != p]
    sibling = [(at(t, c, p), at(t, 1 - c, p)) for t, c, p in spots]
    over_x = [(at(t, c, p), at(t, c, 1 - p)) for t, c, p in spots]
    over_y = [(at(t, c, p), at(t ^ 1, c, p)) for t, c, p in spots]
    cycle = [2 * z for z in range(layers)] + [2 * z + 1 for z in reversed(range(layers))]
    length = len(cycle)
    after = {cycle[i]: cycle[(i + 1) % length] for i in range(length)}
    before = {chip_: source for source, chip_ in after.items()}
    around = [
        (at(t, c, p), at((after if c == 0 else before)[t], c, p)) for t, c, p in spots
    ]

    def place(chip_):
        return jnp.where(chip_ % 2 == 0, chip_ // 2, length - 1 - chip_ // 2)

    pick = local_pick[0, 0]
    owner = owners[0]
    own_chip = owner // 2
    own_here = chip == own_chip
    direct = (owner % 2) == core
    ahead = (place(chip) - place(own_chip) + length) % length
    distance = jnp.where(core == 0, ahead, (length - ahead) % length)

    part = half // 2 // CHUNKS
    chunk_shape = (n_orb, part, grid, grid)
    cut = orbitals.reshape((n_orb, 2, half // 2, grid, grid))

    def of_half(which, lo, hi):
        begin = (0, which, lo * part, 0, 0)
        piece = lax.dynamic_slice(cut, begin, (n_orb, 1, (hi - lo) * part, grid, grid))
        return piece.reshape((n_orb, hi - lo, part, grid, grid))

    first_out, own_first, cut, orbitals = lax.optimization_barrier(
        (of_half(1 - core, 0, 1), of_half(core, 0, 1), cut, orbitals)
    )
    first_in = move(first_out, sibling)
    chosen_orbital = lax.dynamic_index_in_dim(orbitals, pick, 0, keepdims=False)
    rest_in = move(orbitals, sibling).reshape(cut.shape)
    first_in, chosen_orbital, cut = lax.optimization_barrier((first_in, chosen_orbital, cut))
    crossed = move(chosen_orbital, cross)
    fresh = [jnp.where(direct, own_first, first_in)[:, 0]]
    for k in range(1, CHUNKS):
        begin = (0, core, k * part, 0, 0)
        size = (n_orb, 1, part, grid, grid)
        both = [lax.dynamic_slice(v, begin, size)[:, 0] for v in (cut, rest_in)]
        fresh.append(jnp.where(direct, *both))
    info = jnp.stack([core.astype(jnp.int32), distance.astype(jnp.int32)])

    steps = CHUNKS + length - 2
    kept = []

    def arrived(k):
        return pl.pallas_call(
            pick_body,
            in_specs=[pl.BlockSpec(memory_space=pltpu.SMEM)]
            + [pl.BlockSpec(memory_space=pl.ANY)] * length,
            out_specs=pl.BlockSpec(memory_space=pltpu.VMEM),
            out_shape=jax.ShapeDtypeStruct(chunk_shape, F32),
            scratch_shapes=[pltpu.SemaphoreType.DMA],
        )(info, *kept[k : k + length])

    carried, phi = None, None
    flying, swapping = [], []
    owns, others = [], []
    t = 0
    while len(others) < CHUNKS:
        joined = [flying.pop(0)] if flying and flying[0][0] <= t else []
        landed = [swapping.pop(0)] if swapping and swapping[0][0] <= t else []
        values = [] if carried is None else [carried]
        values += [item[1] for item in joined + landed]
        if t == 1:
            values.append(info)
        if t == 2:
            values += fresh[3:]
        if t == PHI_STEP:
            values.append(crossed)
        if t == PHI_STEP + 1:
            values.append(phi)
        if len(values) > 1:
            values = list(lax.optimization_barrier(tuple(values)))
        if t == 2:
            fresh[3:] = values[-len(fresh[3:]) :]
            values = values[: -len(fresh[3:])]
        if t == 1:
            info = values.pop()
        if t == PHI_STEP + 1:
            phi = values.pop()
        if t == PHI_STEP:
            phi = jnp.where(home, chosen_orbital, values.pop())
        if landed:
            others.append(values.pop())
        if joined:
            mine, got = joined[0][2], values.pop()
            owns.append(jnp.where(home, mine, got))
            swapping.append((t + 1, move(jnp.where(home, got, mine), sibling)))
        carried = None
        if t <= steps:
            held = jnp.where(own_here, fresh[t], values[0]) if 0 < t < CHUNKS else (values or fresh)[0]
            kept.append(held)
            if t < steps:
                carried = move(held, around)
        k = t - length + 1
        if 0 <= k < CHUNKS:
            mine = arrived(k)
            flying.append((t + HOP_STEPS, move(mine, over_x), mine))
        t += 1

    planes = 2 * part
    phi = phi.reshape((2, half // 2, grid, grid))
    own = [jnp.stack(owns[lo:hi]) for lo, hi in GROUPS]
    other = [jnp.stack(others[lo:hi]) for lo, hi in GROUPS]
    table = tables(grid, part)

    def whole(shape):
        return pl.BlockSpec(shape, lambda i, info: (0,) * len(shape))

    def chosen(shape):
        return pl.BlockSpec((1,) + shape, lambda i, info: (info[0],) + (0,) * len(shape))

    square = (2 * grid, 2 * grid)

    pairs = pl.BlockSpec((UNITS,) + chunk_shape, lambda i, info: (i, 0, 0, 0, 0))
    lines = pl.BlockSpec((2, half, UNITS * planes, grid), lambda i, info: (0, 0, i, 0))
    keeps, sends = [], []
    for g, (lo, hi) in enumerate(GROUPS):
        spectrum = jax.ShapeDtypeStruct((2, half, (hi - lo) * planes, grid), F32)
        slab = pl.BlockSpec(
            (2, UNITS * part, grid, grid), lambda i, info, lo=lo: (0, lo // UNITS + i, 0, 0)
        )
        keep, send = call(
            forward_body,
            (hi - lo) // UNITS,
            [slab, pairs, pairs] + [whole(square)] * 2 + [chosen(square)] * 2,
            [lines, lines],
            [spectrum, spectrum],
        )(info, phi, own[g], other[g], *table["last_fwd"], *table["mid_fwd"])
        keeps.append(keep)
        sends.append(send)
    recvs = [move(send, sibling) for send in sends]
    cols = [
        pl.BlockSpec((2, MIDDLE_ROWS, (hi - lo) * planes, grid), lambda i, info: (0, i, 0, 0))
        for lo, hi in GROUPS
    ]
    shapes = [jax.ShapeDtypeStruct(keep.shape, F32) for keep in keeps]
    results = call(
        middle_body,
        half // MIDDLE_ROWS,
        cols * 2 + [chosen(square)] * 4,
        cols * 2,
        shapes * 2,
    )(info, *keeps, *recvs, *table["first_fwd"], *table["first_inv"])
    keeps, sends = results[: len(GROUPS)], results[len(GROUPS) :]
    recvs = [move(send, sibling) for send in sends]
    terms = []
    terms = []
    for lo, hi in TERM_GROUPS:
        g, start = [(g, a) for g, (a, b) in enumerate(GROUPS) if a <= lo < b][0]
        keep, recv = keeps[g], recvs[g]
        if len(terms) > 1:
            there, keep = lax.optimization_barrier((terms[-2][1], keep))
            terms[-2] = (terms[-2][0], there)
        shift = (lo - start) // UNITS
        some_lines = pl.BlockSpec(
            (2, half, UNITS * planes, grid), lambda i, info, shift=shift: (0, 0, shift + i, 0)
        )
        some_pairs = pl.BlockSpec(
            (UNITS,) + chunk_shape, lambda i, info, shift=shift: (shift + i, 0, 0, 0, 0)
        )
        term = call(
            backward_body,
            (hi - lo) // UNITS,
            [some_lines, some_lines, some_pairs, some_pairs]
            + [chosen(square)] * 2
            + [whole(square)] * 2,
            pl.BlockSpec((2, UNITS * part, grid, grid), lambda i, info: (0, i, 0, 0)),
            jax.ShapeDtypeStruct((2, (hi - lo) * part, grid, grid), F32),
        )(info, keep, recv, own[g], other[g], *table["mid_inv"], *table["last_inv"])
        terms.append((term, move(term, cross)))
    total = jnp.concatenate([jnp.where(home, *both) for both in terms], axis=1)
    return total.reshape((1, half, grid, grid))


def solution(mesh):
    in_specs = (P("band", "fft", None, None), P(), P("band", None))
    out_specs = P("band", "fft", None, None)
    two_slabs = mesh.shape["fft"] == 2 and mesh.shape["band"] % 4 == 0

    def on_device(orbitals, owners, local_pick):
        fits = (
            orbitals.shape[0] == 2
            and orbitals.shape[1] == CHUNKS * ROWS
            and orbitals.shape[-1] % 128 == 0
            and owners.shape[0] == 1
            and local_pick.shape == (1, 1)
        )
        if two_slabs and fits:
            return paired(orbitals, owners, local_pick)
        return general(orbitals, owners, local_pick)

    return jax.shard_map(
        on_device, mesh=mesh, in_specs=in_specs, out_specs=out_specs, check_vma=False
    )
```

```python
import functools
import math

import jax
import jax.numpy as jnp
import ml_dtypes
import numpy as np
from jax import lax
from jax.experimental import pallas as pl
from jax.experimental.pallas import tpu as pltpu
from jax.sharding import PartitionSpec as P

F32 = jnp.float32
BF16 = jnp.bfloat16
ROWS = 8
CHUNKS = 8
UNITS = 2
MIDDLE_ROWS = 32
GROUPS = ((0, 4), (4, 6), (6, 8))
TERM_GROUPS = ((0, 2), (2, 4), (4, 6), (6, 8))
HOP_STEPS = 2
PHI_STEP = 6


def spread(shard, axis, root):
    mine = lax.axis_index(axis) == root
    return lax.psum(jnp.where(mine, shard, jnp.zeros_like(shard)), axis)


def dft_tables(size):
    index = jnp.arange(size, dtype=jnp.int32)
    product = index[:, None] * index[None, :] % size
    angle = product.astype(jnp.float32) * (2.0 * math.pi / size)
    return (jnp.cos(angle), jnp.sin(angle))


def signed_freq(index, size):
    return jnp.where(index < size // 2, index, index - size).astype(jnp.float32)


def along(form, data, table):
    return jnp.einsum(form, data, table, precision=lax.Precision.HIGHEST)


def transform(density, cosine, sine, kernel):
    last_form = "pzxy,yk->pzxk"
    middle_form = "pzxy,xk->pzky"
    first_form = "pzab,zk->pkab"
    evens = density[0::2]
    odds = density[1::2]
    real_part = along(last_form, evens, cosine) + along(last_form, odds, sine)
    imag_part = along(last_form, odds, cosine) - along(last_form, evens, sine)
    mixed_real = along(middle_form, real_part, cosine) + along(middle_form, imag_part, sine)
    mixed_imag = along(middle_form, imag_part, cosine) - along(middle_form, real_part, sine)
    line_real = lax.all_to_all(mixed_real, "fft", split_axis=2, concat_axis=1, tiled=True)
    line_imag = lax.all_to_all(mixed_imag, "fft", split_axis=2, concat_axis=1, tiled=True)
    spec_real = along(first_form, line_real, cosine) + along(first_form, line_imag, sine)
    spec_imag = along(first_form, line_imag, cosine) - along(first_form, line_real, sine)
    spec_real = spec_real * kernel
    spec_imag = spec_imag * kernel
    back_real = along(first_form, spec_real, cosine) - along(first_form, spec_imag, sine)
    back_imag = along(first_form, spec_imag, cosine) + along(first_form, spec_real, sine)
    slab_real = lax.all_to_all(back_real, "fft", split_axis=1, concat_axis=2, tiled=True)
    slab_imag = lax.all_to_all(back_imag, "fft", split_axis=1, concat_axis=2, tiled=True)
    inner_real = along(middle_form, slab_real, cosine) - along(middle_form, slab_imag, sine)
    inner_imag = along(middle_form, slab_imag, cosine) + along(middle_form, slab_real, sine)
    first_field = along(last_form, inner_real, cosine) - along(last_form, inner_imag, sine)
    second_field = along(last_form, inner_imag, cosine) + along(last_form, inner_real, sine)
    return jnp.stack([first_field, second_field], 1).reshape(density.shape)


def general(orbitals, owners, local_pick):
    grid = orbitals.shape[-1]
    cosine, sine = dft_tables(grid)
    groups = lax.axis_size("fft")
    width = grid // groups
    start = lax.axis_index("fft") * width
    freq_first = signed_freq(jnp.arange(grid, dtype=jnp.int32), grid)
    freq_second = signed_freq(start + jnp.arange(width, dtype=jnp.int32), grid)
    square = (
        freq_first[:, None, None] ** 2
        + freq_second[None, :, None] ** 2
        + freq_first[None, None, :] ** 2
    )
    scale = 0.25 * grid * math.sqrt(grid) / (grid * grid * grid)
    kernel = jnp.where(square > 0, scale / jnp.maximum(square, 1.0), 0.0)
    selected = jnp.take(orbitals, local_pick[0], axis=0)
    grid_shape = selected.shape[1:]
    total = jnp.zeros_like(selected)
    for step in range(owners.shape[0]):
        sent = spread(orbitals, "band", owners[step])
        density = (sent[:, None] * selected[None]).reshape((-1,) + grid_shape)
        potentials = transform(density, cosine, sine, kernel)
        shaped = potentials.reshape((sent.shape[0], selected.shape[0]) + grid_shape)
        total = total + jnp.sum(shaped * sent[:, None], axis=0)
    return total


def host_tables(grid):
    index = np.arange(grid)
    angle = 2.0 * np.pi * (np.outer(index, index) % grid) / grid
    return np.cos(angle), np.sin(angle)


def as_pair(table):
    high = table.astype(ml_dtypes.bfloat16)
    low = (table - high.astype(np.float64)).astype(ml_dtypes.bfloat16)
    return jnp.asarray(high), jnp.asarray(low)


def blocks(a, b, c, d):
    return np.block([[a, b], [c, d]])


def plane_order(core, half, part):
    base = np.arange(half).reshape(2, -1, part)
    if core:
        base = base[::-1]
    return core * half + base.transpose(1, 0, 2).reshape(-1)


def tables(grid, part):
    cos, sin = host_tables(grid)
    half = grid // 2
    columns = [np.arange(grid), np.concatenate([np.arange(half, grid), np.arange(half)])]
    slabs = [plane_order(core, half, part) for core in range(2)]
    depths = [np.concatenate([slabs[core], slabs[1 - core]]) for core in range(2)]

    def to_spectrum(order):
        c, s = cos[order], sin[order]
        return blocks(c, s, -s, c)

    def from_planes(order):
        c, s = cos[:, order], sin[:, order]
        return blocks(c, s, -s, c)

    def to_planes(order):
        c, s = cos[order], sin[order]
        return blocks(c, -s, s, c)

    def from_spectrum(order):
        c, s = cos[:, order], sin[:, order]
        return blocks(c, -s, s, c)

    both = dict(
        last_fwd=blocks(cos, -sin, sin, cos),
        last_inv=blocks(cos, sin, -sin, cos),
        mid_fwd=np.stack([to_spectrum(order) for order in columns]),
        mid_inv=np.stack([from_spectrum(order) for order in columns]),
        first_fwd=np.stack([from_planes(order) for order in depths]),
        first_inv=np.stack([to_planes(order) for order in depths]),
    )
    return {name: as_pair(value) for name, value in both.items()}


def split(value):
    high = value.astype(BF16)
    return high, (value - high.astype(F32)).astype(BF16)


def mm(a, b):
    return jnp.dot(a, b, preferred_element_type=F32)


def right(data, high, low):
    top, rest = split(data)
    return mm(top, high) + (mm(rest, high) + mm(top, low))


def left(high, low, data):
    top, rest = split(data)
    return mm(high, top) + (mm(high, rest) + mm(low, top))


def pick_body(info, *refs):
    inputs, out, sem = refs[:-2], refs[-2], refs[-1]
    for index, ref in enumerate(inputs):

        @pl.when(info[1] == index)
        def _(ref=ref):
            pltpu.make_async_copy(ref, out, sem).start()

    pltpu.make_async_copy(inputs[0], out, sem).wait()


def forward_body(info, phi, *refs):
    units = (len(refs) - 6) // 2
    own, other = refs[:units], refs[units : 2 * units]
    wyh, wyl, wxh, wxl, keep, send = refs[2 * units :]
    grid = phi.shape[-1]
    half = grid // 2
    part = phi.shape[1]
    rows = 2 * part
    core = info[0]
    part = part // units
    re, im = [], []
    for u in range(units):
        near = phi[core, u * part : (u + 1) * part]
        far = phi[1 - core, u * part : (u + 1) * part]
        re += [near * own[u][0, 0], far * other[u][0, 0]]
        im += [near * own[u][0, 1], far * other[u][0, 1]]
    re = jnp.concatenate(re, axis=0)
    im = jnp.concatenate(im, axis=0)
    data = jnp.concatenate([re, im], axis=-1).reshape(rows * grid, 2 * grid)
    lines = right(data, wyh[...], wyl[...])
    for first in range(0, rows, 2):
        planes = []
        for z in (first, first + 1):
            plane = lines[z * grid : (z + 1) * grid]
            planes.append(jnp.concatenate([plane[:, :grid], plane[:, grid:]], axis=0))
        out = left(wxh[0], wxl[0], jnp.concatenate(planes, axis=1))
        for pos, z in enumerate((first, first + 1)):
            plane = out[:, pos * grid : (pos + 1) * grid]
            for comp in range(2):
                base = comp * grid
                keep[comp, :, z, :] = plane[base : base + half]
                send[comp, :, z, :] = plane[base + half : base + grid]


def middle_body(info, *refs):
    count = (len(refs) - 4) // 4
    keeps, recvs = refs[:count], refs[count : 2 * count]
    wfh, wfl, wih, wil = refs[2 * count : 2 * count + 4]
    keep_outs, send_outs = refs[2 * count + 4 : 3 * count + 4], refs[3 * count + 4 :]
    rows = keeps[0].shape[1]
    grid = keeps[0].shape[-1]
    half = grid // 2
    scale = 0.25 * grid * math.sqrt(grid) / (grid * grid * grid)
    kz = lax.broadcasted_iota(jnp.int32, (grid, grid), 0)
    ky = lax.broadcasted_iota(jnp.int32, (grid, grid), 1)
    fz = jnp.where(kz < grid // 2, kz, kz - grid)
    fy = jnp.where(ky < grid // 2, ky, ky - grid)
    plane_square = fz * fz + fy * fy
    start = info[0] * half + pl.program_id(0) * rows
    lane = lax.broadcasted_iota(jnp.int32, (1, grid), 1)
    for first in range(0, rows, 2):
        planes = []
        for k in (first, first + 1):
            for comp in range(2):
                pieces = [ref[comp, k] for ref in keeps + recvs]
                if k == 0:
                    drop = jnp.where((lane == 0) & (start == 0), pieces[0][0:1], 0.0)
                    pieces = [piece - drop for piece in pieces]
                planes.append(jnp.concatenate(pieces, axis=0))
        data = jnp.concatenate(
            [
                jnp.concatenate(planes[:2], axis=0),
                jnp.concatenate(planes[2:], axis=0),
            ],
            axis=1,
        )
        spec = left(wfh[0], wfl[0], data)
        factors = []
        for k in (first, first + 1):
            kx = start + k
            fx = jnp.where(kx < grid // 2, kx, kx - grid)
            square = (plane_square + fx * fx).astype(F32)
            factors.append(jnp.where(square > 0, scale / jnp.maximum(square, 1.0), 0.0))
        factor = jnp.concatenate(factors, axis=1)
        spec = spec * jnp.concatenate([factor, factor], axis=0)
        out = left(wih[0], wil[0], spec)
        for pos, k in enumerate((first, first + 1)):
            plane = out[:, pos * grid : (pos + 1) * grid]
            for comp in range(2):
                row = comp * grid
                for ref in keep_outs + send_outs:
                    size = ref.shape[2]
                    ref[comp, k] = plane[row : row + size]
                    row += size


def backward_body(info, keep, recv, *refs):
    units = (len(refs) - 5) // 2
    own, other = refs[:units], refs[units : 2 * units]
    wxh, wxl, wyh, wyl, out = refs[2 * units :]
    grid = keep.shape[-1]
    rows = keep.shape[2]
    part = rows // 2 // units
    core = info[0]
    lines = []
    for first in range(0, rows, 2):
        planes = []
        for z in (first, first + 1):
            planes.append(
                jnp.concatenate(
                    [keep[0, :, z, :], recv[0, :, z, :], keep[1, :, z, :], recv[1, :, z, :]],
                    axis=0,
                )
            )
        mixed = left(wxh[0], wxl[0], jnp.concatenate(planes, axis=1))
        for pos in range(2):
            plane = mixed[:, pos * grid : (pos + 1) * grid]
            lines.append(jnp.concatenate([plane[:grid], plane[grid:]], axis=1))
    fields = right(jnp.concatenate(lines, axis=0), wyh[...], wyl[...])
    re = fields[:, :grid].reshape(rows, grid, grid)
    im = fields[:, grid:].reshape(rows, grid, grid)
    for u in range(units):
        near = slice(2 * u * part, (2 * u + 1) * part)
        far = slice((2 * u + 1) * part, (2 * u + 2) * part)
        place = pl.ds(u * part, part)
        out[core, place] = re[near] * own[u][0, 0] + im[near] * own[u][0, 1]
        out[1 - core, place] = re[far] * other[u][0, 0] + im[far] * other[u][0, 1]


def call(body, grid_size, in_specs, out_specs, out_shape):
    return pl.pallas_call(
        body,
        grid_spec=pltpu.PrefetchScalarGridSpec(
            num_scalar_prefetch=1,
            grid=(grid_size,),
            in_specs=in_specs,
            out_specs=out_specs,
        ),
        out_shape=out_shape,
        compiler_params=pltpu.CompilerParams(vmem_limit_bytes=32 * 1024 * 1024),
    )


def paired(orbitals, owners, local_pick):
    n_orb, half, grid, _ = orbitals.shape
    bands = lax.axis_size("band")
    chips = bands // 2
    layers = chips // 2
    band = lax.axis_index("band")
    x = lax.axis_index("fft")
    core = band % 2
    chip = band // 2
    y = chip % 2
    home = core == x
    axes = ("band", "fft")

    def at(chip_, core_, x_):
        return (chip_ * 2 + core_) * 2 + x_

    def move(value, pairs):
        return lax.ppermute(value, axes, pairs)

    spots = [(t, c, p) for t in range(chips) for c in range(2) for p in range(2)]
    cross = [(at(t, c, p), at(t, p, c)) for t, c, p in spots if c != p]
    sibling = [(at(t, c, p), at(t, 1 - c, p)) for t, c, p in spots]
    over_x = [(at(t, c, p), at(t, c, 1 - p)) for t, c, p in spots]
    over_y = [(at(t, c, p), at(t ^ 1, c, p)) for t, c, p in spots]
    cycle = [2 * z for z in range(layers)] + [2 * z + 1 for z in reversed(range(layers))]
    length = len(cycle)
    after = {cycle[i]: cycle[(i + 1) % length] for i in range(length)}
    before = {chip_: source for source, chip_ in after.items()}
    around = [
        (at(t, c, p), at((after if c == 0 else before)[t], c, p)) for t, c, p in spots
    ]

    def place(chip_):
        return jnp.where(chip_ % 2 == 0, chip_ // 2, length - 1 - chip_ // 2)

    pick = local_pick[0, 0]
    owner = owners[0]
    own_chip = owner // 2
    own_here = chip == own_chip
    direct = (owner % 2) == core
    ahead = (place(chip) - place(own_chip) + length) % length
    distance = jnp.where(core == 0, ahead, (length - ahead) % length)

    part = half // 2 // CHUNKS
    chunk_shape = (n_orb, part, grid, grid)
    cut = orbitals.reshape((n_orb, 2, half // 2, grid, grid))

    def of_half(which, lo, hi):
        begin = (0, which, lo * part, 0, 0)
        piece = lax.dynamic_slice(cut, begin, (n_orb, 1, (hi - lo) * part, grid, grid))
        return piece.reshape((n_orb, hi - lo, part, grid, grid))

    first_out, own_first, cut, orbitals = lax.optimization_barrier(
        (of_half(1 - core, 0, 1), of_half(core, 0, 1), cut, orbitals)
    )
    first_in = move(first_out, sibling)
    chosen_orbital = lax.dynamic_index_in_dim(orbitals, pick, 0, keepdims=False)
    rest_in = move(orbitals, sibling).reshape(cut.shape)
    first_in, chosen_orbital, cut = lax.optimization_barrier((first_in, chosen_orbital, cut))
    crossed = move(chosen_orbital, cross)
    fresh = [jnp.where(direct, own_first, first_in)[:, 0]]
    for k in range(1, CHUNKS):
        begin = (0, core, k * part, 0, 0)
        size = (n_orb, 1, part, grid, grid)
        both = [lax.dynamic_slice(v, begin, size)[:, 0] for v in (cut, rest_in)]
        fresh.append(jnp.where(direct, *both))
    info = jnp.stack([core.astype(jnp.int32), distance.astype(jnp.int32)])

    steps = CHUNKS + length - 2
    kept = []

    def arrived(k):
        return pl.pallas_call(
            pick_body,
            in_specs=[pl.BlockSpec(memory_space=pltpu.SMEM)]
            + [pl.BlockSpec(memory_space=pl.ANY)] * length,
            out_specs=pl.BlockSpec(memory_space=pltpu.VMEM),
            out_shape=jax.ShapeDtypeStruct(chunk_shape, F32),
            scratch_shapes=[pltpu.SemaphoreType.DMA],
        )(info, *kept[k : k + length])

    carried, phi = None, None
    flying, swapping = [], []
    owns, others = [], []
    t = 0
    while len(others) < CHUNKS:
        joined = [flying.pop(0)] if flying and flying[0][0] <= t else []
        landed = [swapping.pop(0)] if swapping and swapping[0][0] <= t else []
        values = [] if carried is None else [carried]
        values += [item[1] for item in joined + landed]
        if t == 1:
            values.append(info)
        if t == 2:
            values += fresh[3:]
        if t == PHI_STEP:
            values.append(crossed)
        if t == PHI_STEP + 1:
            values.append(phi)
        if len(values) > 1:
            values = list(lax.optimization_barrier(tuple(values)))
        if t == 2:
            fresh[3:] = values[-len(fresh[3:]) :]
            values = values[: -len(fresh[3:])]
        if t == 1:
            info = values.pop()
        if t == PHI_STEP + 1:
            phi = values.pop()
        if t == PHI_STEP:
            phi = jnp.where(home, chosen_orbital, values.pop())
        if landed:
            others.append(values.pop())
        if joined:
            mine, got = joined[0][2], values.pop()
            owns.append(jnp.where(home, mine, got))
            swapping.append((t + 1, move(jnp.where(home, got, mine), sibling)))
        carried = None
        if t <= steps:
            held = jnp.where(own_here, fresh[t], values[0]) if 0 < t < CHUNKS else (values or fresh)[0]
            kept.append(held)
            if t < steps:
                carried = move(held, around)
        k = t - length + 1
        if 0 <= k < CHUNKS:
            mine = arrived(k)
            flying.append((t + HOP_STEPS, move(mine, over_x), mine))
        t += 1

    planes = 2 * part
    phi = phi.reshape((2, half // 2, grid, grid))

    def by_unit(values, lo, hi):
        if hi - lo == UNITS:
            return [value[None] for value in values[lo:hi]]
        return [jnp.stack(values[lo:hi])] * UNITS

    own = [by_unit(owns, lo, hi) for lo, hi in GROUPS]
    other = [by_unit(others, lo, hi) for lo, hi in GROUPS]
    table = tables(grid, part)

    def whole(shape):
        return pl.BlockSpec(shape, lambda i, info: (0,) * len(shape))

    def chosen(shape):
        return pl.BlockSpec((1,) + shape, lambda i, info: (info[0],) + (0,) * len(shape))

    square = (2 * grid, 2 * grid)


    def unit_specs(shift):
        return [
            pl.BlockSpec(
                (1,) + chunk_shape,
                lambda i, info, u=u: ((shift + i) * UNITS + u if shift is not None else 0, 0, 0, 0, 0),
            )
            for u in range(UNITS)
        ]

    lines = pl.BlockSpec((2, half, UNITS * planes, grid), lambda i, info: (0, 0, i, 0))
    keeps, sends = [], []
    for g, (lo, hi) in enumerate(GROUPS):
        spectrum = jax.ShapeDtypeStruct((2, half, (hi - lo) * planes, grid), F32)
        slab = pl.BlockSpec(
            (2, UNITS * part, grid, grid), lambda i, info, lo=lo: (0, lo // UNITS + i, 0, 0)
        )
        keep, send = call(
            forward_body,
            (hi - lo) // UNITS,
            [slab] + unit_specs(0 if hi - lo > UNITS else None) * 2 + [whole(square)] * 2 + [chosen(square)] * 2,
            [lines, lines],
            [spectrum, spectrum],
        )(info, phi, *own[g], *other[g], *table["last_fwd"], *table["mid_fwd"])
        keeps.append(keep)
        sends.append(send)
    recvs = [move(send, sibling) for send in sends]
    cols = [
        pl.BlockSpec((2, MIDDLE_ROWS, (hi - lo) * planes, grid), lambda i, info: (0, i, 0, 0))
        for lo, hi in GROUPS
    ]
    shapes = [jax.ShapeDtypeStruct(keep.shape, F32) for keep in keeps]
    results = call(
        middle_body,
        half // MIDDLE_ROWS,
        cols * 2 + [chosen(square)] * 4,
        cols * 2,
        shapes * 2,
    )(info, *keeps, *recvs, *table["first_fwd"], *table["first_inv"])
    keeps, sends = results[: len(GROUPS)], results[len(GROUPS) :]
    recvs = [move(send, sibling) for send in sends]
    terms = []
    terms = []
    for lo, hi in TERM_GROUPS:
        g, start = [(g, a) for g, (a, b) in enumerate(GROUPS) if a <= lo < b][0]
        keep, recv = keeps[g], recvs[g]
        if len(terms) > 1:
            there, keep = lax.optimization_barrier((terms[-2][1], keep))
            terms[-2] = (terms[-2][0], there)
        shift = (lo - start) // UNITS
        some_lines = pl.BlockSpec(
            (2, half, UNITS * planes, grid), lambda i, info, shift=shift: (0, 0, shift + i, 0)
        )
        g_units = unit_specs(shift if GROUPS[g][1] - GROUPS[g][0] > UNITS else None)
        term = call(
            backward_body,
            (hi - lo) // UNITS,
            [some_lines, some_lines] + g_units * 2
            + [chosen(square)] * 2
            + [whole(square)] * 2,
            pl.BlockSpec((2, UNITS * part, grid, grid), lambda i, info: (0, i, 0, 0)),
            jax.ShapeDtypeStruct((2, (hi - lo) * part, grid, grid), F32),
        )(info, keep, recv, *own[g], *other[g], *table["mid_inv"], *table["last_inv"])
        terms.append((term, move(term, cross)))
    total = jnp.concatenate([jnp.where(home, *both) for both in terms], axis=1)
    return total.reshape((1, half, grid, grid))


def solution(mesh):
    in_specs = (P("band", "fft", None, None), P(), P("band", None))
    out_specs = P("band", "fft", None, None)
    two_slabs = mesh.shape["fft"] == 2 and mesh.shape["band"] % 4 == 0

    def on_device(orbitals, owners, local_pick):
        fits = (
            orbitals.shape[0] == 2
            and orbitals.shape[1] == CHUNKS * ROWS
            and orbitals.shape[-1] % 128 == 0
            and owners.shape[0] == 1
            and local_pick.shape == (1, 1)
        )
        if two_slabs and fits:
            return paired(orbitals, owners, local_pick)
        return general(orbitals, owners, local_pick)

    return jax.shard_map(
        on_device, mesh=mesh, in_specs=in_specs, out_specs=out_specs, check_vma=False
    )
```

```python
import functools
import math

import jax
import jax.numpy as jnp
import ml_dtypes
import numpy as np
from jax import lax
from jax.experimental import pallas as pl
from jax.experimental.pallas import tpu as pltpu
from jax.sharding import PartitionSpec as P

F32 = jnp.float32
BF16 = jnp.bfloat16
ROWS = 8
CHUNKS = 8
UNITS = 2
MIDDLE_ROWS = 32
GROUPS = ((0, 4), (4, 6), (6, 8))
TERM_GROUPS = ((0, 2), (2, 4), (4, 6), (6, 8))
HOP_STEPS = 2
PHI_STEP = 5


def spread(shard, axis, root):
    mine = lax.axis_index(axis) == root
    return lax.psum(jnp.where(mine, shard, jnp.zeros_like(shard)), axis)


def dft_tables(size):
    index = jnp.arange(size, dtype=jnp.int32)
    product = index[:, None] * index[None, :] % size
    angle = product.astype(jnp.float32) * (2.0 * math.pi / size)
    return (jnp.cos(angle), jnp.sin(angle))


def signed_freq(index, size):
    return jnp.where(index < size // 2, index, index - size).astype(jnp.float32)


def along(form, data, table):
    return jnp.einsum(form, data, table, precision=lax.Precision.HIGHEST)


def transform(density, cosine, sine, kernel):
    last_form = "pzxy,yk->pzxk"
    middle_form = "pzxy,xk->pzky"
    first_form = "pzab,zk->pkab"
    evens = density[0::2]
    odds = density[1::2]
    real_part = along(last_form, evens, cosine) + along(last_form, odds, sine)
    imag_part = along(last_form, odds, cosine) - along(last_form, evens, sine)
    mixed_real = along(middle_form, real_part, cosine) + along(middle_form, imag_part, sine)
    mixed_imag = along(middle_form, imag_part, cosine) - along(middle_form, real_part, sine)
    line_real = lax.all_to_all(mixed_real, "fft", split_axis=2, concat_axis=1, tiled=True)
    line_imag = lax.all_to_all(mixed_imag, "fft", split_axis=2, concat_axis=1, tiled=True)
    spec_real = along(first_form, line_real, cosine) + along(first_form, line_imag, sine)
    spec_imag = along(first_form, line_imag, cosine) - along(first_form, line_real, sine)
    spec_real = spec_real * kernel
    spec_imag = spec_imag * kernel
    back_real = along(first_form, spec_real, cosine) - along(first_form, spec_imag, sine)
    back_imag = along(first_form, spec_imag, cosine) + along(first_form, spec_real, sine)
    slab_real = lax.all_to_all(back_real, "fft", split_axis=1, concat_axis=2, tiled=True)
    slab_imag = lax.all_to_all(back_imag, "fft", split_axis=1, concat_axis=2, tiled=True)
    inner_real = along(middle_form, slab_real, cosine) - along(middle_form, slab_imag, sine)
    inner_imag = along(middle_form, slab_imag, cosine) + along(middle_form, slab_real, sine)
    first_field = along(last_form, inner_real, cosine) - along(last_form, inner_imag, sine)
    second_field = along(last_form, inner_imag, cosine) + along(last_form, inner_real, sine)
    return jnp.stack([first_field, second_field], 1).reshape(density.shape)


def general(orbitals, owners, local_pick):
    grid = orbitals.shape[-1]
    cosine, sine = dft_tables(grid)
    groups = lax.axis_size("fft")
    width = grid // groups
    start = lax.axis_index("fft") * width
    freq_first = signed_freq(jnp.arange(grid, dtype=jnp.int32), grid)
    freq_second = signed_freq(start + jnp.arange(width, dtype=jnp.int32), grid)
    square = (
        freq_first[:, None, None] ** 2
        + freq_second[None, :, None] ** 2
        + freq_first[None, None, :] ** 2
    )
    scale = 0.25 * grid * math.sqrt(grid) / (grid * grid * grid)
    kernel = jnp.where(square > 0, scale / jnp.maximum(square, 1.0), 0.0)
    selected = jnp.take(orbitals, local_pick[0], axis=0)
    grid_shape = selected.shape[1:]
    total = jnp.zeros_like(selected)
    for step in range(owners.shape[0]):
        sent = spread(orbitals, "band", owners[step])
        density = (sent[:, None] * selected[None]).reshape((-1,) + grid_shape)
        potentials = transform(density, cosine, sine, kernel)
        shaped = potentials.reshape((sent.shape[0], selected.shape[0]) + grid_shape)
        total = total + jnp.sum(shaped * sent[:, None], axis=0)
    return total


def host_tables(grid):
    index = np.arange(grid)
    angle = 2.0 * np.pi * (np.outer(index, index) % grid) / grid
    return np.cos(angle), np.sin(angle)


def as_pair(table):
    high = table.astype(ml_dtypes.bfloat16)
    low = (table - high.astype(np.float64)).astype(ml_dtypes.bfloat16)
    return jnp.asarray(high), jnp.asarray(low)


def blocks(a, b, c, d):
    return np.block([[a, b], [c, d]])


def plane_order(core, half, part):
    base = np.arange(half).reshape(2, -1, part)
    if core:
        base = base[::-1]
    return core * half + base.transpose(1, 0, 2).reshape(-1)


def tables(grid, part):
    cos, sin = host_tables(grid)
    half = grid // 2
    columns = [np.arange(grid), np.concatenate([np.arange(half, grid), np.arange(half)])]
    slabs = [plane_order(core, half, part) for core in range(2)]
    depths = [np.concatenate([slabs[core], slabs[1 - core]]) for core in range(2)]

    def to_spectrum(order):
        c, s = cos[order], sin[order]
        return blocks(c, s, -s, c)

    def from_planes(order):
        c, s = cos[:, order], sin[:, order]
        return blocks(c, s, -s, c)

    def to_planes(order):
        c, s = cos[order], sin[order]
        return blocks(c, -s, s, c)

    def from_spectrum(order):
        c, s = cos[:, order], sin[:, order]
        return blocks(c, -s, s, c)

    both = dict(
        last_fwd=blocks(cos, -sin, sin, cos),
        last_inv=blocks(cos, sin, -sin, cos),
        mid_fwd=np.stack([to_spectrum(order) for order in columns]),
        mid_inv=np.stack([from_spectrum(order) for order in columns]),
        first_fwd=np.stack([from_planes(order) for order in depths]),
        first_inv=np.stack([to_planes(order) for order in depths]),
    )
    return {name: as_pair(value) for name, value in both.items()}


def split(value):
    high = value.astype(BF16)
    return high, (value - high.astype(F32)).astype(BF16)


def mm(a, b):
    return jnp.dot(a, b, preferred_element_type=F32)


def right(data, high, low):
    top, rest = split(data)
    return mm(top, high) + (mm(rest, high) + mm(top, low))


def left(high, low, data):
    top, rest = split(data)
    return mm(high, top) + (mm(high, rest) + mm(low, top))


def pick_body(info, *refs):
    inputs, out, sem = refs[:-2], refs[-2], refs[-1]
    for index, ref in enumerate(inputs):

        @pl.when(info[1] == index)
        def _(ref=ref):
            pltpu.make_async_copy(ref, out, sem).start()

    pltpu.make_async_copy(inputs[0], out, sem).wait()


def forward_body(info, phi, *refs):
    units = (len(refs) - 6) // 2
    own, other = refs[:units], refs[units : 2 * units]
    wyh, wyl, wxh, wxl, keep, send = refs[2 * units :]
    grid = phi.shape[-1]
    half = grid // 2
    part = phi.shape[1]
    rows = 2 * part
    core = info[0]
    part = part // units
    re, im = [], []
    for u in range(units):
        near = phi[core, u * part : (u + 1) * part]
        far = phi[1 - core, u * part : (u + 1) * part]
        re += [near * own[u][0, 0], far * other[u][0, 0]]
        im += [near * own[u][0, 1], far * other[u][0, 1]]
    re = jnp.concatenate(re, axis=0)
    im = jnp.concatenate(im, axis=0)
    data = jnp.concatenate([re, im], axis=-1).reshape(rows * grid, 2 * grid)
    lines = right(data, wyh[...], wyl[...])
    for first in range(0, rows, 2):
        planes = []
        for z in (first, first + 1):
            plane = lines[z * grid : (z + 1) * grid]
            planes.append(jnp.concatenate([plane[:, :grid], plane[:, grid:]], axis=0))
        out = left(wxh[0], wxl[0], jnp.concatenate(planes, axis=1))
        for pos, z in enumerate((first, first + 1)):
            plane = out[:, pos * grid : (pos + 1) * grid]
            for comp in range(2):
                base = comp * grid
                keep[comp, :, z, :] = plane[base : base + half]
                send[comp, :, z, :] = plane[base + half : base + grid]


def middle_body(info, *refs):
    count = (len(refs) - 4) // 4
    keeps, recvs = refs[:count], refs[count : 2 * count]
    wfh, wfl, wih, wil = refs[2 * count : 2 * count + 4]
    keep_outs, send_outs = refs[2 * count + 4 : 3 * count + 4], refs[3 * count + 4 :]
    rows = keeps[0].shape[1]
    grid = keeps[0].shape[-1]
    half = grid // 2
    scale = 0.25 * grid * math.sqrt(grid) / (grid * grid * grid)
    kz = lax.broadcasted_iota(jnp.int32, (grid, grid), 0)
    ky = lax.broadcasted_iota(jnp.int32, (grid, grid), 1)
    fz = jnp.where(kz < grid // 2, kz, kz - grid)
    fy = jnp.where(ky < grid // 2, ky, ky - grid)
    plane_square = fz * fz + fy * fy
    start = info[0] * half + pl.program_id(0) * rows
    lane = lax.broadcasted_iota(jnp.int32, (1, grid), 1)
    for first in range(0, rows, 2):
        planes = []
        for k in (first, first + 1):
            for comp in range(2):
                pieces = [ref[comp, k] for ref in keeps + recvs]
                if k == 0:
                    drop = jnp.where((lane == 0) & (start == 0), pieces[0][0:1], 0.0)
                    pieces = [piece - drop for piece in pieces]
                planes.append(jnp.concatenate(pieces, axis=0))
        data = jnp.concatenate(
            [
                jnp.concatenate(planes[:2], axis=0),
                jnp.concatenate(planes[2:], axis=0),
            ],
            axis=1,
        )
        spec = left(wfh[0], wfl[0], data)
        factors = []
        for k in (first, first + 1):
            kx = start + k
            fx = jnp.where(kx < grid // 2, kx, kx - grid)
            square = (plane_square + fx * fx).astype(F32)
            factors.append(jnp.where(square > 0, scale / jnp.maximum(square, 1.0), 0.0))
        factor = jnp.concatenate(factors, axis=1)
        spec = spec * jnp.concatenate([factor, factor], axis=0)
        out = left(wih[0], wil[0], spec)
        for pos, k in enumerate((first, first + 1)):
            plane = out[:, pos * grid : (pos + 1) * grid]
            for comp in range(2):
                row = comp * grid
                for ref in keep_outs + send_outs:
                    size = ref.shape[2]
                    ref[comp, k] = plane[row : row + size]
                    row += size


def backward_body(info, keep, recv, *refs):
    units = (len(refs) - 5) // 2
    own, other = refs[:units], refs[units : 2 * units]
    wxh, wxl, wyh, wyl, out = refs[2 * units :]
    grid = keep.shape[-1]
    rows = keep.shape[2]
    part = rows // 2 // units
    core = info[0]
    lines = []
    for first in range(0, rows, 2):
        planes = []
        for z in (first, first + 1):
            planes.append(
                jnp.concatenate(
                    [keep[0, :, z, :], recv[0, :, z, :], keep[1, :, z, :], recv[1, :, z, :]],
                    axis=0,
                )
            )
        mixed = left(wxh[0], wxl[0], jnp.concatenate(planes, axis=1))
        for pos in range(2):
            plane = mixed[:, pos * grid : (pos + 1) * grid]
            lines.append(jnp.concatenate([plane[:grid], plane[grid:]], axis=1))
    fields = right(jnp.concatenate(lines, axis=0), wyh[...], wyl[...])
    re = fields[:, :grid].reshape(rows, grid, grid)
    im = fields[:, grid:].reshape(rows, grid, grid)
    for u in range(units):
        near = slice(2 * u * part, (2 * u + 1) * part)
        far = slice((2 * u + 1) * part, (2 * u + 2) * part)
        place = pl.ds(u * part, part)
        out[core, place] = re[near] * own[u][0, 0] + im[near] * own[u][0, 1]
        out[1 - core, place] = re[far] * other[u][0, 0] + im[far] * other[u][0, 1]


def call(body, grid_size, in_specs, out_specs, out_shape):
    return pl.pallas_call(
        body,
        grid_spec=pltpu.PrefetchScalarGridSpec(
            num_scalar_prefetch=1,
            grid=(grid_size,),
            in_specs=in_specs,
            out_specs=out_specs,
        ),
        out_shape=out_shape,
        compiler_params=pltpu.CompilerParams(vmem_limit_bytes=32 * 1024 * 1024),
    )


def paired(orbitals, owners, local_pick):
    n_orb, half, grid, _ = orbitals.shape
    bands = lax.axis_size("band")
    chips = bands // 2
    layers = chips // 2
    band = lax.axis_index("band")
    x = lax.axis_index("fft")
    core = band % 2
    chip = band // 2
    y = chip % 2
    home = core == x
    axes = ("band", "fft")

    def at(chip_, core_, x_):
        return (chip_ * 2 + core_) * 2 + x_

    def move(value, pairs):
        return lax.ppermute(value, axes, pairs)

    spots = [(t, c, p) for t in range(chips) for c in range(2) for p in range(2)]
    cross = [(at(t, c, p), at(t, p, c)) for t, c, p in spots if c != p]
    sibling = [(at(t, c, p), at(t, 1 - c, p)) for t, c, p in spots]
    over_x = [(at(t, c, p), at(t, c, 1 - p)) for t, c, p in spots]
    over_y = [(at(t, c, p), at(t ^ 1, c, p)) for t, c, p in spots]
    cycle = [2 * z for z in range(layers)] + [2 * z + 1 for z in reversed(range(layers))]
    length = len(cycle)
    after = {cycle[i]: cycle[(i + 1) % length] for i in range(length)}
    before = {chip_: source for source, chip_ in after.items()}
    around = [
        (at(t, c, p), at((after if c == 0 else before)[t], c, p)) for t, c, p in spots
    ]

    def place(chip_):
        return jnp.where(chip_ % 2 == 0, chip_ // 2, length - 1 - chip_ // 2)

    pick = local_pick[0, 0]
    owner = owners[0]
    own_chip = owner // 2
    own_here = chip == own_chip
    direct = (owner % 2) == core
    ahead = (place(chip) - place(own_chip) + length) % length
    distance = jnp.where(core == 0, ahead, (length - ahead) % length)

    part = half // 2 // CHUNKS
    chunk_shape = (n_orb, part, grid, grid)
    cut = orbitals.reshape((n_orb, 2, half // 2, grid, grid))

    def of_half(which, lo, hi):
        begin = (0, which, lo * part, 0, 0)
        piece = lax.dynamic_slice(cut, begin, (n_orb, 1, (hi - lo) * part, grid, grid))
        return piece.reshape((n_orb, hi - lo, part, grid, grid))

    first_out, own_first, cut, orbitals = lax.optimization_barrier(
        (of_half(1 - core, 0, 1), of_half(core, 0, 1), cut, orbitals)
    )
    first_in = move(first_out, sibling)
    chosen_orbital = lax.dynamic_index_in_dim(orbitals, pick, 0, keepdims=False)
    rest_in = move(orbitals, sibling).reshape(cut.shape)
    first_in, chosen_orbital, cut = lax.optimization_barrier((first_in, chosen_orbital, cut))
    crossed = move(chosen_orbital, cross)
    fresh = [jnp.where(direct, own_first, first_in)[:, 0]]
    for k in range(1, CHUNKS):
        begin = (0, core, k * part, 0, 0)
        size = (n_orb, 1, part, grid, grid)
        both = [lax.dynamic_slice(v, begin, size)[:, 0] for v in (cut, rest_in)]
        fresh.append(jnp.where(direct, *both))
    info = jnp.stack([core.astype(jnp.int32), distance.astype(jnp.int32)])

    steps = CHUNKS + length - 2
    kept = []

    def arrived(k):
        return pl.pallas_call(
            pick_body,
            in_specs=[pl.BlockSpec(memory_space=pltpu.SMEM)]
            + [pl.BlockSpec(memory_space=pl.ANY)] * length,
            out_specs=pl.BlockSpec(memory_space=pltpu.VMEM),
            out_shape=jax.ShapeDtypeStruct(chunk_shape, F32),
            scratch_shapes=[pltpu.SemaphoreType.DMA],
        )(info, *kept[k : k + length])

    carried, phi = None, None
    flying, swapping = [], []
    owns, others = [], []
    t = 0
    while len(others) < CHUNKS:
        joined = [flying.pop(0)] if flying and flying[0][0] <= t else []
        landed = [swapping.pop(0)] if swapping and swapping[0][0] <= t else []
        values = [] if carried is None else [carried]
        values += [item[1] for item in joined + landed]
        if t == 1:
            values.append(info)
        if t == 2:
            values += fresh[3:]
        if t == PHI_STEP:
            values.append(crossed)
        if t == PHI_STEP + 1:
            values.append(phi)
        if len(values) > 1:
            values = list(lax.optimization_barrier(tuple(values)))
        if t == 2:
            fresh[3:] = values[-len(fresh[3:]) :]
            values = values[: -len(fresh[3:])]
        if t == 1:
            info = values.pop()
        if t == PHI_STEP + 1:
            phi = values.pop()
        if t == PHI_STEP:
            phi = jnp.where(home, chosen_orbital, values.pop())
        if landed:
            others.append(values.pop())
        if joined:
            mine, got = joined[0][2], values.pop()
            owns.append(jnp.where(home, mine, got))
            swapping.append((t + 1, move(jnp.where(home, got, mine), sibling)))
        carried = None
        if t <= steps:
            held = jnp.where(own_here, fresh[t], values[0]) if 0 < t < CHUNKS else (values or fresh)[0]
            kept.append(held)
            if t < steps:
                carried = move(held, around)
        k = t - length + 1
        if 0 <= k < CHUNKS:
            mine = arrived(k)
            flying.append((t + HOP_STEPS, move(mine, over_x), mine))
        t += 1

    planes = 2 * part
    phi = phi.reshape((2, half // 2, grid, grid))

    def by_unit(values, lo, hi):
        if hi - lo == UNITS:
            return [value[None] for value in values[lo:hi]]
        return [jnp.stack(values[lo:hi])] * UNITS

    own = [by_unit(owns, lo, hi) for lo, hi in GROUPS]
    other = [by_unit(others, lo, hi) for lo, hi in GROUPS]
    table = tables(grid, part)

    def whole(shape):
        return pl.BlockSpec(shape, lambda i, info: (0,) * len(shape))

    def chosen(shape):
        return pl.BlockSpec((1,) + shape, lambda i, info: (info[0],) + (0,) * len(shape))

    square = (2 * grid, 2 * grid)


    def unit_specs(shift):
        return [
            pl.BlockSpec(
                (1,) + chunk_shape,
                lambda i, info, u=u: ((shift + i) * UNITS + u if shift is not None else 0, 0, 0, 0, 0),
            )
            for u in range(UNITS)
        ]

    lines = pl.BlockSpec((2, half, UNITS * planes, grid), lambda i, info: (0, 0, i, 0))
    keeps, sends = [], []
    for g, (lo, hi) in enumerate(GROUPS):
        spectrum = jax.ShapeDtypeStruct((2, half, (hi - lo) * planes, grid), F32)
        slab = pl.BlockSpec(
            (2, UNITS * part, grid, grid), lambda i, info, lo=lo: (0, lo // UNITS + i, 0, 0)
        )
        keep, send = call(
            forward_body,
            (hi - lo) // UNITS,
            [slab] + unit_specs(0 if hi - lo > UNITS else None) * 2 + [whole(square)] * 2 + [chosen(square)] * 2,
            [lines, lines],
            [spectrum, spectrum],
        )(info, phi, *own[g], *other[g], *table["last_fwd"], *table["mid_fwd"])
        keeps.append(keep)
        sends.append(send)
    recvs = [move(send, sibling) for send in sends]
    cols = [
        pl.BlockSpec((2, MIDDLE_ROWS, (hi - lo) * planes, grid), lambda i, info: (0, i, 0, 0))
        for lo, hi in GROUPS
    ]
    shapes = [jax.ShapeDtypeStruct(keep.shape, F32) for keep in keeps]
    results = call(
        middle_body,
        half // MIDDLE_ROWS,
        cols * 2 + [chosen(square)] * 4,
        cols * 2,
        shapes * 2,
    )(info, *keeps, *recvs, *table["first_fwd"], *table["first_inv"])
    keeps, sends = results[: len(GROUPS)], results[len(GROUPS) :]
    recvs = [move(send, sibling) for send in sends]
    terms = []
    terms = []
    for lo, hi in TERM_GROUPS:
        g, start = [(g, a) for g, (a, b) in enumerate(GROUPS) if a <= lo < b][0]
        keep, recv = keeps[g], recvs[g]
        if len(terms) > 1:
            there, keep = lax.optimization_barrier((terms[-2][1], keep))
            terms[-2] = (terms[-2][0], there)
        shift = (lo - start) // UNITS
        some_lines = pl.BlockSpec(
            (2, half, UNITS * planes, grid), lambda i, info, shift=shift: (0, 0, shift + i, 0)
        )
        g_units = unit_specs(shift if GROUPS[g][1] - GROUPS[g][0] > UNITS else None)
        term = call(
            backward_body,
            (hi - lo) // UNITS,
            [some_lines, some_lines] + g_units * 2
            + [chosen(square)] * 2
            + [whole(square)] * 2,
            pl.BlockSpec((2, UNITS * part, grid, grid), lambda i, info: (0, i, 0, 0)),
            jax.ShapeDtypeStruct((2, (hi - lo) * part, grid, grid), F32),
        )(info, keep, recv, *own[g], *other[g], *table["mid_inv"], *table["last_inv"])
        terms.append((term, move(term, cross)))
    total = jnp.concatenate([jnp.where(home, *both) for both in terms], axis=1)
    return total.reshape((1, half, grid, grid))


def solution(mesh):
    in_specs = (P("band", "fft", None, None), P(), P("band", None))
    out_specs = P("band", "fft", None, None)
    two_slabs = mesh.shape["fft"] == 2 and mesh.shape["band"] % 4 == 0

    def on_device(orbitals, owners, local_pick):
        fits = (
            orbitals.shape[0] == 2
            and orbitals.shape[1] == CHUNKS * ROWS
            and orbitals.shape[-1] % 128 == 0
            and owners.shape[0] == 1
            and local_pick.shape == (1, 1)
        )
        if two_slabs and fits:
            return paired(orbitals, owners, local_pick)
        return general(orbitals, owners, local_pick)

    return jax.shard_map(
        on_device, mesh=mesh, in_specs=in_specs, out_specs=out_specs, check_vma=False
    )
```
